512 devices in a mesh: dp: 4 (over x), expert: 128 (over y, z, core).
Axes of the slice: x: 4, y: 4, z: 16, core: 2. Of those that a mesh axis runs over, the one named last changes fastest.
Arguments:
- grads: bfloat16 [65536, 1024], P(('dp', 'expert')), may hold values from -6 to 6
- route_weight: float32 [65536, 8], P(('dp', 'expert')), may hold values from 0.1 to 1
- routes: int32 [65536, 8], P(('dp', 'expert')), may hold values from 0 to 127, all different within a row; in each aligned block of 128 rows (0 to 127, 128 to 255, ...) at most 12 rows name the same one
- hot: int32 [128], replicated, may hold values from 0 to 1, as said below
- expert_inputs: bfloat16 [4, 128, 128, 1, 2, 4, 768], P('dp', 'expert'), may hold values from -6 to 6
Outputs:
- input_factor: float32 [768, 128, 768], P('dp', 'expert')
- grad_factor: float32 [1024, 128, 1024], P('dp', 'expert')
The draws below stay inside these ranges and needn't reach their ends.
Inputs may be any that keep to these rules, and one draw needn't show every extreme that they name: `routes`: within each device's 128 tokens no expert is chosen more than 3 * 4 times, and some expert exactly that often. Every expert e with e >= 64 has hot[e] = 1; the others have a replica or not.
All inputs are finite; a program needn't handle non-finite values.
Results may differ from the reference program's by a relative error of at most 0.013.
Values may be sent and summed in bfloat16 or wider, within the bound.
A program may use at most 64 MiB of HBM per device.

```python
import math
import jax
import jax.numpy as jnp
import numpy as np
from jax import lax

FF = 768
DW = 1024
EXPERTS = 128
TOP = 8
TOK_DEV = 128
EXP_DEV = 1
CAP = 4
TOKENS = 65536
ROWS_EXP = 4096
N_DP = 4
N_EXPERT = 128


def draw_hot(key, part):
    key = jax.random.fold_in(key, 11)
    coins = jax.random.randint(key, (EXPERTS,), 0, 2).astype(jnp.int32)
    owner = jnp.arange(EXPERTS, dtype=jnp.int32) // EXP_DEV
    return jnp.where(owner >= N_EXPERT // 2, 1, coins).astype(jnp.int32)


def block_levels(rng, dims, shards, smallest, high):
    gain = 1.0
    for dim, blocks in shards:
        draws = jax.random.uniform(jax.random.fold_in(jax.random.fold_in(rng, 6), dim), (blocks,), jnp.float32, smallest / len(shards), high / len(shards))
        gain = gain * jnp.repeat(jnp.exp(draws), dims[dim] // blocks).reshape((-1,) + (1,) * (len(dims) - 1 - dim))
    return gain


def assign_block(stream_key, own, number, rows, amount, top, limit, lean):
    ranking = jax.random.permutation(stream_key, amount)
    packed, ordinary = shares(amount, rows * top, limit, lean, True), shares(amount, rows * top, limit, lean, False)
    places = jnp.arange(amount)

    def named(tallies, turn):
        used = int((tallies > 0).sum())
        fixed = max(1, used // 4)
        passed = fixed + (places - fixed + turn * (used - fixed)) % max(1, amount - fixed)
        return jnp.zeros((amount,), jnp.int32).at[ranking[jnp.where(places < fixed, places, passed)]].set(jnp.asarray(tallies, jnp.int32))

    tallies = jnp.where(number % 4 == 0, named(packed, number // 4), named(ordinary, number - number // 4 - 1))
    mixed = jax.random.permutation(jax.random.fold_in(own, 3), amount)
    source_of, taker = mixed[0:amount // 2 * 2:2], mixed[1:amount // 2 * 2:2]
    slack = jnp.minimum(tallies[source_of] - 1, limit - tallies[taker]) // 2
    slack = jnp.where((source_of == ranking[0]) | (taker == ranking[0]) | (tallies[taker] == 0), 0, jnp.maximum(slack, 0))
    passed = jax.random.randint(jax.random.fold_in(own, 4), (amount // 2,), 0, 1 << 20) % (slack + 1)
    tallies = tallies.at[source_of].add(-passed).at[taker].add(passed)
    items = jnp.searchsorted(jnp.cumsum(tallies), jnp.arange(rows * top), side="right").astype(jnp.int32)
    listing = items.reshape(top, rows).T
    listing = listing[jax.random.permutation(jax.random.fold_in(own, 1), rows)]
    turn = jax.random.randint(jax.random.fold_in(own, 2), (rows, 1), 0, top)
    return jnp.take_along_axis(listing, (jnp.arange(top)[None, :] + turn) % top, axis=1)


def shares(count, total, bound, lean, full):
    portions = [(1 << 20) // math.isqrt(standing ** lean) + 1 for standing in range(1, count + 1)]
    largest = bound if full else min(bound, max(-(-total // count), total * portions[0] // sum(portions)))
    least = 1 if total - largest >= count - 1 else 0
    holding, rest = [largest] + [least] * (count - 1), total - largest - least * (count - 1)
    while rest > 0:
        free = [i for i in range(1, count) if holding[i] < largest] or [i for i in range(1, count) if holding[i] < bound]
        pool, left = sum([portions[i] for i in free]), rest
        for i in free:
            more = min(bound - holding[i], max(1, left * portions[i] // pool), rest)
            holding[i] = holding[i] + more
            rest = rest - more
    return np.array(holding)


def gaussian(key, shape, width, reach, pieces=(), kind=jnp.bfloat16):
    values = jax.random.normal(key, shape, jnp.float32) * width
    if len(pieces) > 0:
        values = block_levels(key, shape, pieces, -0.22, 0.18) * values
    return jnp.clip(values, min=-reach, max=reach).astype(kind)


def setup_inputs(seed: int = 0) -> dict:
    arg_keys = jax.random.split(jax.random.key(seed), 6)
    grads = gaussian(arg_keys[0], (TOKENS, DW), 1.0, 6.0, ((0, 512),))
    route_weight = jnp.clip(jnp.exp(math.log(1.0) - 2.3025851 * jax.random.uniform(arg_keys[1], (TOKENS, TOP), jnp.float32) ** block_levels(arg_keys[1], (TOKENS, TOP), ((0, 512),), -0.2, 0.2)), 0.1, 1.0)
    routes_keys = jax.random.split(jax.random.fold_in(arg_keys[2], 1), TOKENS // TOK_DEV)
    routes_turns = jax.random.permutation(jax.random.fold_in(arg_keys[2], 3), TOKENS // TOK_DEV)
    routes = jax.vmap(lambda own, number: assign_block(jax.random.fold_in(arg_keys[2], 2), own, number, TOK_DEV, EXPERTS, TOP, 3 * CAP, 2))(routes_keys, routes_turns).reshape((TOKENS, TOP))
    hot = draw_hot(jax.random.fold_in(arg_keys[5], 71), 0)
    expert_inputs = gaussian(arg_keys[4], (N_DP, N_EXPERT, N_EXPERT, EXP_DEV, 2, CAP, FF), 1.0, 6.0, ((0, 4), (1, 128)))
    return {"grads": grads, "route_weight": route_weight, "routes": routes, "hot": hot, "expert_inputs": expert_inputs}


def rounded(value):
    return lax.optimization_barrier(value.astype(jnp.bfloat16)).astype(jnp.float32)


def reference(grads, route_weight, routes, hot, expert_inputs):
    n_src = N_DP * N_EXPERT
    half = N_EXPERT // 2
    blocks = routes.reshape(n_src, TOK_DEV, TOP)
    labels = jnp.arange(EXPERTS, dtype=jnp.int32)
    counts = jnp.zeros((n_src, TOK_DEV, EXPERTS), jnp.int32)
    for which in range(TOP):
        counts = counts + (blocks[:, :, which, None] == labels).astype(jnp.int32)
    before = jnp.cumsum(counts, axis=1) - counts
    rank = jnp.take_along_axis(before, blocks, axis=2).astype(jnp.int32)
    is_hot = hot[blocks] == 1
    own = rank < CAP
    spill = (rank >= CAP) & (rank < 2 * CAP) & is_hot
    owner = blocks // EXP_DEV
    local = blocks % EXP_DEV
    dest = jnp.where(own, owner, jnp.bitwise_xor(owner, half))
    part = jnp.where(own, 0, 1)
    slot = jnp.where(own, rank, rank - CAP)
    source = jnp.arange(n_src, dtype=jnp.int32)[:, None, None]
    src_dp = source // N_EXPERT
    src_n = source % N_EXPERT
    flat = ((((src_dp * N_EXPERT + dest) * EXP_DEV + local) * 2 + part) * N_EXPERT + src_n) * CAP + slot
    total = N_DP * N_EXPERT * EXP_DEV * 2 * N_EXPERT * CAP
    index = jnp.where(own | spill, flat, total).reshape(-1)
    tok_ids = jnp.broadcast_to(source * TOK_DEV + jnp.arange(TOK_DEV, dtype=jnp.int32)[None, :, None], blocks.shape).reshape(-1)
    pick_ids = jnp.broadcast_to(jnp.arange(TOP, dtype=jnp.int32)[None, None, :], blocks.shape).reshape(-1)
    shape6 = (N_DP, N_EXPERT, EXP_DEV, 2, N_EXPERT, CAP)
    table_tok = jnp.zeros((total,), jnp.int32).at[index].set(tok_ids, mode="drop").reshape(shape6)
    table_pick = jnp.zeros((total,), jnp.int32).at[index].set(pick_ids, mode="drop").reshape(shape6)
    table_on = jnp.zeros((total,), jnp.int32).at[index].set(1, mode="drop").reshape(shape6)

    def grad_rows(tok, pick, occupied):
        weight = route_weight[tok, pick]
        rows = (weight[..., None] * grads[tok].astype(jnp.float32)).astype(jnp.bfloat16).astype(jnp.float32)
        return rows * occupied[..., None].astype(jnp.float32)

    def gram(rows):
        return jnp.einsum("irf,irg->ifg", rows, rows, precision=lax.Precision.HIGHEST)

    def one_expert(expert):
        owner_dev = expert // EXP_DEV
        slot_l = expert % EXP_DEV
        host = jnp.bitwise_xor(owner_dev, half)
        rows_own = grad_rows(table_tok[:, owner_dev, slot_l, 0], table_pick[:, owner_dev, slot_l, 0], table_on[:, owner_dev, slot_l, 0])
        rows_rep = grad_rows(table_tok[:, host, slot_l, 1], table_pick[:, host, slot_l, 1], table_on[:, host, slot_l, 1])
        in_own = expert_inputs[:, owner_dev, :, slot_l, 0].astype(jnp.float32) * table_on[:, owner_dev, slot_l, 0][..., None].astype(jnp.float32)
        in_rep = expert_inputs[:, host, :, slot_l, 1].astype(jnp.float32) * table_on[:, host, slot_l, 1][..., None].astype(jnp.float32)
        in_rep_g = rounded(gram(in_rep.reshape(N_DP, -1, FF)))
        grad_rep_g = rounded(gram(rows_rep.reshape(N_DP, -1, DW)))
        in_part = (gram(in_own.reshape(N_DP, -1, FF)) + in_rep_g).astype(jnp.bfloat16)
        grad_part = (gram(rows_own.reshape(N_DP, -1, DW)) + grad_rep_g).astype(jnp.bfloat16)
        return jnp.sum(in_part.astype(jnp.float32), axis=0), jnp.sum(grad_part.astype(jnp.float32), axis=0)

    in_sums, grad_sums = lax.map(one_expert, jnp.arange(EXPERTS, dtype=jnp.int32))
    factor = 1.0 / ROWS_EXP
    return jnp.transpose(in_sums * factor, (1, 0, 2)), jnp.transpose(grad_sums * factor, (1, 0, 2))
```

```python
import jax
import jax.numpy as jnp
from jax import lax
from jax.experimental import pallas as pl
from jax.experimental.pallas import tpu as pltpu
from jax.sharding import PartitionSpec as P

NY, NZ, NC, NX = 4, 16, 2, 4
GROUP = NY * NC
HALF = NZ // 2
TOK, TOP, EXPERTS, CAP = 128, 8, 128, 4
WIDTH, HIDDEN = 1024, 768
SLOTS = 2 * CAP
F32, BF16 = jnp.float32, jnp.bfloat16
TN = (((0,), (0,)), ((), ()))


def mm(a, b):
    return jnp.dot(a, b, preferred_element_type=F32)


def iota(shape, dim):
    return lax.broadcasted_iota(jnp.int32, shape, dim)


def kernel(
    routes_ref, weight_ref, hot_ref, grads_ref, inputs_ref,
    grad_out, input_out,
    tokens, table, table_l, table_r, far_inputs, counts, counts_in,
    rows_out, rows_in, gram_g, gram_x,
    gs_out, gs_via, gs_l, gs_r, xs_out, xs_via, xs_l, xs_r,
    tok_send, tok_recv, tab_send, tab_recv, far_sem, cnt_send, cnt_recv,
    row_send, row_recv, gsem_s, gsem_r, xsem_s, xsem_r,
):
    x = lax.axis_index("dp")
    n = lax.axis_index("expert")
    core = lax.rem(n, NC)
    z = lax.rem(n // NC, NZ)
    y = n // (NC * NZ)
    j = y * NC + core

    def expert_at(yy, zz, cc):
        return (yy * NZ + zz) * NC + cc

    z_up = (x, expert_at(y, lax.rem(z + 1, NZ), core))
    z_down = (x, expert_at(y, lax.rem(z + NZ - 1, NZ), core))
    x_up = (lax.rem(x + 1, NX), n)
    x_down = (lax.rem(x + NX - 1, NX), n)

    def flip(k):
        ky, kc = k // NC, k % NC
        if ky == 0:
            yy = y
        elif ky == 1:
            yy = y + 1 - 2 * lax.rem(y, 2)
        elif ky == 2:
            yy = lax.rem(y + 2, 4)
        else:
            yy = 3 - y
        cc = core if kc == 0 else 1 - core
        return yy, cc

    def group_dev(k):
        yy, cc = flip(k)
        return (x, expert_at(yy, z, cc))

    def group_pos(k):
        yy, cc = flip(k)
        return yy * NC + cc

    partners = [z_up, z_down, x_up, x_down] + [group_dev(k) for k in range(1, GROUP)]

    def remote(src, dst, ssem, rsem, dev):
        return pltpu.make_async_remote_copy(
            src_ref=src, dst_ref=dst, send_sem=ssem, recv_sem=rsem,
            device_id=dev, device_id_type=pl.DeviceIdType.MESH,
        )

    barrier = pltpu.get_barrier_semaphore()
    for dev in partners:
        pl.semaphore_signal(barrier, inc=1, device_id=dev, device_id_type=pl.DeviceIdType.MESH)
    pl.semaphore_wait(barrier, len(partners))

    pending = []

    def start(copy):
        copy.start()
        pending.append(copy)
        return copy

    H = TOK // 2

    def token_copy(step, up, half):
        lo = half * H
        base = 0 if up else TOK
        if step == 1:
            src = grads_ref.at[pl.ds(lo, H)]
        else:
            src = tokens.at[step - 2, pl.ds(base + lo, H)]
        if step == HALF:
            dst = tokens.at[HALF - 1, pl.ds(TOK + lo, H)]
        else:
            dst = tokens.at[step - 1, pl.ds(base + lo, H)]
        d = 0 if up else 1
        return remote(
            src, dst, tok_send.at[d, step - 1, half], tok_recv.at[d, step - 1, half],
            z_up if up else z_down,
        )

    tok = {}
    for step in range(1, HALF):
        for half in range(2):
            for up in (True, False):
                tok[step, up, half] = token_copy(step, up, half)
    tok[HALF, True, 0] = token_copy(HALF, True, 0)
    tok[HALF, False, 1] = token_copy(HALF, False, 1)

    def table_copy(step, up):
        buf = table_l if up else table_r
        src = table if step == 1 else buf.at[step - 2]
        d = 0 if up else 1
        return remote(
            src, buf.at[step - 1], tab_send.at[d, step - 1], tab_recv.at[d, step - 1],
            z_up if up else z_down,
        )

    tab = {(s, up): table_copy(s, up) for s in range(1, HALF + 1) for up in (True, False)
           if s < HALF or up}

    for half in range(2):
        for up in (True, False):
            start(tok[1, up, half])

    chosen = routes_ref[...]
    erow = iota((EXPERTS, TOK), 0)
    tcol = iota((EXPERTS, TOK), 1)
    onehot = jnp.zeros((EXPERTS, TOK), F32)
    for k in range(TOP):
        onehot += jnp.where(erow == chosen[k:k + 1, :], 1.0, 0.0)
    earlier = jnp.where(erow < tcol, 1.0, 0.0).astype(BF16)
    before = mm(onehot.astype(BF16), earlier)
    hot = jnp.sum(jnp.where(erow == tcol, jnp.broadcast_to(hot_ref[...].astype(F32), (EXPERTS, TOK)), 0.0),
                  axis=1, keepdims=True)
    limit = jnp.where(hot > 0.5, float(SLOTS), float(CAP))
    ranked = jnp.where(before < limit, before, 1000.0)
    places = []
    for k in range(TOP):
        rank = jnp.sum(jnp.where(erow == chosen[k:k + 1, :], ranked, 0.0), axis=0, keepdims=True)
        slot = chosen[k:k + 1, :].astype(F32) * float(SLOTS) + rank
        places.append(jnp.where(rank < 100.0, slot, -1.0))
    table[0:TOP, :] = jnp.concatenate(places, axis=0)
    table[TOP:2 * TOP, :] = weight_ref[...]

    def pass_table(step):
        for up in (True, False):
            if (step, up) in tab:
                start(tab[step, up])

    def got_table(step):
        for up in (True, False):
            if (step, up) in tab:
                tab[step, up].wait_recv()

    pass_table(1)
    far = start(remote(inputs_ref.at[1], far_inputs, far_sem.at[0], far_sem.at[1], group_dev(4)))

    def advance_table(step):
        got_table(step)
        if step < HALF:
            pass_table(step + 1)

    def advance_tokens(step):
        for half in range(2):
            for up in (True, False):
                if (step, up, half) in tok:
                    tok[step, up, half].wait_recv()
                    if (step + 1, up, half) in tok:
                        start(tok[step + 1, up, half])

    ri = iota((GROUP * 2 * SLOTS, TOK), 0)
    rj = ri // (2 * SLOTS)
    rsrc = lax.rem(ri // SLOTS, 2)
    rslot = (rj // NC) * (NZ * NC * SLOTS) + z * (NC * SLOTS) + lax.rem(rj, NC) * SLOTS + lax.rem(ri, SLOTS)
    want_l = jnp.where(rsrc == 0, rslot, -5).astype(F32)
    want_r = jnp.where(rsrc == 1, rslot, -5).astype(F32)

    def pick(tbl, want):
        sel = jnp.zeros(want.shape, F32)
        wgt = jnp.zeros(want.shape, F32)
        for k in range(TOP):
            hit = want == tbl[k:k + 1, :]
            sel = jnp.where(hit, 1.0, sel)
            wgt = jnp.where(hit, tbl[TOP + k:TOP + k + 1, :], wgt)
        return sel.astype(BF16), wgt

    def dispatch(pair):
        if pair == HALF - 1:
            t_l, t_r = table[...], table_l[HALF - 1]
            g_l = grads_ref[...]
        else:
            t_l, t_r = table_l[pair], table_r[pair]
            g_l = tokens[pair, 0:TOK]
        g_r = tokens[pair, TOK:2 * TOK]
        s_l, w_l = pick(t_l, want_l)
        s_r, w_r = pick(t_r, want_r)
        weight = jnp.sum(w_l + w_r, axis=1, keepdims=True)
        rows = ((mm(s_l, g_l) + mm(s_r, g_r)) * weight).astype(BF16)
        rows_out[pair] = rows.reshape(GROUP, 2 * SLOTS, WIDTH)
        for k in (4, 5, 2, 3, 6, 7, 1):
            start(row_copy(pair, k))
        rows_in[pair, 0] = rows_out[pair, j]

    def row_copy(pair, k):
        return remote(rows_out.at[pair, group_pos(k)], rows_in.at[pair, k],
                      row_send.at[pair, k], row_recv.at[pair, k], group_dev(k))

    def send_counts():
        def one(tbl, zz):
            for jj in range(GROUP):
                lo = (((jj // NC) * NZ + z) * NC + jj % NC) * SLOTS
                lo = lo.astype(F32)
                hit = (tbl >= lo) & (tbl < lo + float(SLOTS))
                counts[jj, pl.ds(zz, 1), :] = jnp.sum(jnp.where(hit, 1.0, 0.0), axis=0, keepdims=True)

        one(table[0:TOP, :], z)
        for s in range(1, HALF + 1):
            one(table_l[s - 1, 0:TOP, :], lax.rem(z + NZ - s, NZ))
            if s < HALF:
                one(table_r[s - 1, 0:TOP, :], lax.rem(z + s, NZ))
        for k in range(1, GROUP):
            start(cnt_copy(k))
        counts_in[j] = counts[j]

    def cnt_copy(k):
        return remote(counts.at[group_pos(k)], counts_in.at[j], cnt_send.at[k], cnt_recv.at[k], group_dev(k))

    def input_gram():
        for k in range(1, GROUP):
            cnt_copy(k).wait_recv()
        per = counts_in[...].reshape(EXPERTS, TOK).astype(BF16)
        ones = jnp.ones((TOK, TOK), BF16)
        total = mm(per, ones).astype(BF16)
        rr = EXPERTS * CAP
        spread = jnp.where(iota((rr, EXPERTS), 0) // CAP == iota((rr, EXPERTS), 1), 1.0, 0.0).astype(BF16)
        mine = mm(spread, total)
        slot = lax.rem(iota((rr, TOK), 0), CAP).astype(F32)
        keep_a = jnp.where(mine > slot, 1.0, 0.0).astype(BF16)
        keep_b = jnp.where(mine > slot + float(CAP), 1.0, 0.0).astype(BF16)
        far.wait_recv()
        block = 256
        for i in range(HIDDEN // block):
            cols = pl.ds(i * block, block)
            ka = jnp.concatenate([keep_a] * (block // TOK), axis=1)
            kb = jnp.concatenate([keep_b] * (block // TOK), axis=1)
            gram_x[cols, :] = lax.dot_general(
                inputs_ref[0, :, cols] * ka, inputs_ref[0], TN, preferred_element_type=F32
            ) + lax.dot_general(far_inputs[:, cols] * kb, far_inputs[...], TN, preferred_element_type=F32)

    class Scatter:
        def __init__(self, gram, rows, out, via, l_in, r_in, ssem, rsem):
            self.gram, self.rows, self.out, self.via = gram, rows, out, via
            self.l_in, self.r_in, self.ssem, self.rsem = l_in, r_in, ssem, rsem
            self.h = rows // 2

        def part(self, blk, half):
            at = pl.multiple_of(blk * self.rows + half * self.h, 32)
            return self.gram[pl.ds(at, self.h), :]

        def copies(self):
            h = self.h
            lo, hi = pl.ds(0, h), pl.ds(h, h)
            ends = [
                (self.via.at[0], x_up), (self.via.at[1], x_down),
                (self.l_in.at[hi], x_up), (self.r_in.at[lo], x_down),
                (self.l_in.at[lo], x_up), (self.r_in.at[hi], x_down),
            ]
            return [remote(self.out.at[i], dst, self.ssem.at[i], self.rsem.at[i], dev)
                    for i, (dst, dev) in enumerate(ends)]

        def first(self):
            self.c = self.copies()
            opposite = lax.rem(x + 2, NX)
            nxt, prv = lax.rem(x + 1, NX), lax.rem(x + NX - 1, NX)
            self.out[0] = self.part(opposite, 0).astype(BF16)
            start(self.c[0])
            self.out[1] = self.part(opposite, 1).astype(BF16)
            start(self.c[1])
            self.out[2] = self.part(nxt, 1).astype(BF16)
            start(self.c[2])
            self.out[3] = self.part(prv, 0).astype(BF16)
            start(self.c[3])

        def second(self):
            nxt, prv = lax.rem(x + 1, NX), lax.rem(x + NX - 1, NX)
            self.c[0].wait_recv()
            self.out[4] = (self.part(nxt, 0) + self.via[0].astype(F32)).astype(BF16)
            start(self.c[4])
            self.c[1].wait_recv()
            self.out[5] = (self.part(prv, 1) + self.via[1].astype(F32)).astype(BF16)
            start(self.c[5])

        def last(self, result):
            factor = 1.0 / (TOK * TOP * NX)
            h = self.h
            lo, hi = pl.ds(0, h), pl.ds(h, h)
            self.c[2].wait_recv()
            self.c[3].wait_recv()
            self.c[4].wait_recv()
            result[lo, :] = (self.part(x, 0) + self.l_in[lo].astype(F32) + self.r_in[lo].astype(F32)) * factor
            self.c[5].wait_recv()
            result[hi, :] = (self.part(x, 1) + self.l_in[hi].astype(F32) + self.r_in[hi].astype(F32)) * factor

    xs = Scatter(gram_x, HIDDEN // NX, xs_out, xs_via, xs_l, xs_r, xsem_s, xsem_r)
    gs = Scatter(gram_g, WIDTH // NX, gs_out, gs_via, gs_l, gs_r, gsem_s, gsem_r)

    def gram_part(first_pair, pairs, fresh):
        for p in range(first_pair, first_pair + pairs):
            for k in range(1, GROUP):
                row_copy(p, k).wait_recv()
        kk = pairs * GROUP * 2 * SLOTS

        def body(i, carry):
            at = pl.multiple_of(i * 256, 256)
            a = rows_in[first_pair:first_pair + pairs, :, :, pl.ds(at, 256)].reshape(kk, 256)
            b = rows_in[first_pair:first_pair + pairs].reshape(kk, WIDTH)
            r = lax.dot_general(a, b, TN, preferred_element_type=F32)
            if fresh:
                gram_g[pl.ds(at, 256), :] = r
            else:
                gram_g[pl.ds(at, 256), :] += r
            return carry

        lax.fori_loop(0, WIDTH // 256, body, 0)

    advance_table(1)
    advance_table(2)
    advance_table(3)
    advance_tokens(1)
    advance_table(4)
    advance_table(5)
    advance_table(6)
    advance_tokens(2)
    dispatch(0)
    advance_table(7)
    advance_table(8)
    send_counts()
    advance_tokens(3)
    dispatch(1)
    advance_tokens(4)
    dispatch(2)
    input_gram()
    xs.first()
    advance_tokens(5)
    dispatch(3)
    gram_part(0, 2, True)
    advance_tokens(6)
    xs.second()
    dispatch(4)
    advance_tokens(7)
    dispatch(5)
    gram_part(2, 2, False)
    xs.last(input_out)
    dispatch(6)
    gram_part(4, 2, False)
    advance_tokens(8)
    dispatch(7)
    gram_part(6, 2, False)
    gs.first()
    gs.second()
    gs.last(grad_out)
    for copy in pending:
        copy.wait_send()


def shards(grads, route_weight, routes, hot, expert_inputs):
    inputs = expert_inputs.reshape(NY, NZ, NC, 2, CAP, HIDDEN)
    inputs = inputs.transpose(3, 0, 2, 1, 4, 5).reshape(2, EXPERTS * CAP, HIDDEN)
    vmem = pl.BlockSpec(memory_space=pltpu.VMEM)
    dma = pltpu.SemaphoreType.DMA
    hg, hx = WIDTH // NX // 2, HIDDEN // NX // 2
    grad_rows, input_rows = pl.pallas_call(
        kernel,
        out_shape=(
            jax.ShapeDtypeStruct((WIDTH // NX, WIDTH), F32),
            jax.ShapeDtypeStruct((HIDDEN // NX, HIDDEN), F32),
        ),
        in_specs=[vmem] * 5,
        out_specs=(vmem, vmem),
        scratch_shapes=[
            pltpu.VMEM((HALF, 2 * TOK, WIDTH), BF16),
            pltpu.VMEM((2 * TOP, TOK), F32),
            pltpu.VMEM((HALF, 2 * TOP, TOK), F32),
            pltpu.VMEM((HALF, 2 * TOP, TOK), F32),
            pltpu.VMEM((EXPERTS * CAP, HIDDEN), BF16),
            pltpu.VMEM((GROUP, NZ, TOK), F32),
            pltpu.VMEM((GROUP, NZ, TOK), F32),
            pltpu.VMEM((HALF, GROUP, 2 * SLOTS, WIDTH), BF16),
            pltpu.VMEM((HALF, GROUP, 2 * SLOTS, WIDTH), BF16),
            pltpu.VMEM((WIDTH, WIDTH), F32),
            pltpu.VMEM((HIDDEN, HIDDEN), F32),
            pltpu.VMEM((6, hg, WIDTH), BF16),
            pltpu.VMEM((2, hg, WIDTH), BF16),
            pltpu.VMEM((2 * hg, WIDTH), BF16),
            pltpu.VMEM((2 * hg, WIDTH), BF16),
            pltpu.VMEM((6, hx, HIDDEN), BF16),
            pltpu.VMEM((2, hx, HIDDEN), BF16),
            pltpu.VMEM((2 * hx, HIDDEN), BF16),
            pltpu.VMEM((2 * hx, HIDDEN), BF16),
            dma((2, HALF, 2)), dma((2, HALF, 2)),
            dma((2, HALF)), dma((2, HALF)),
            dma((2,)),
            dma((GROUP,)), dma((GROUP,)),
            dma((HALF, GROUP)), dma((HALF, GROUP)),
            dma((6,)), dma((6,)), dma((6,)), dma((6,)),
        ],
        compiler_params=pltpu.CompilerParams(
            collective_id=0, has_side_effects=True, vmem_limit_bytes=48 * 1024 * 1024
        ),
    )(routes.T, route_weight.T, hot.reshape(1, EXPERTS), grads, inputs)
    return input_rows[:, None, :], grad_rows[:, None, :]


def solution(mesh):
    return jax.shard_map(
        shards,
        mesh=mesh,
        in_specs=(
            P(("dp", "expert"), None),
            P(("dp", "expert"), None),
            P(("dp", "expert"), None),
            P(),
            P("dp", "expert", None, None, None, None, None),
        ),
        out_specs=(P("dp", "expert", None), P("dp", "expert", None)),
        check_vma=False,
    )
```

```python
import jax
import jax.numpy as jnp
from jax import lax
from jax.experimental import pallas as pl
from jax.experimental.pallas import tpu as pltpu
from jax.sharding import PartitionSpec as P

NY, NZ, NC, NX = 4, 16, 2, 4
GROUP = NY * NC
HALF = NZ // 2
TOK, TOP, EXPERTS, CAP = 128, 8, 128, 4
WIDTH, HIDDEN = 1024, 768
SLOTS = 2 * CAP
F32, BF16 = jnp.float32, jnp.bfloat16
TN = (((0,), (0,)), ((), ()))


def mm(a, b):
    return jnp.dot(a, b, preferred_element_type=F32)


def iota(shape, dim):
    return lax.broadcasted_iota(jnp.int32, shape, dim)


def kernel(
    routes_ref, weight_ref, hot_ref, grads_ref, inputs_ref,
    grad_out, input_out,
    tokens, table, table_in, keep, counts, counts_in,
    rows_out, rows_in, gram_g, gram_o, gram_r, mine, theirs,
    gs_out, gs_via, gs_l, gs_r, os_out, os_via, os_l, os_r, rs_out, rs_via, rs_l, rs_r,
    tok_send, tok_recv, tab_send, tab_recv, far_sem, cnt_send, cnt_recv,
    row_send, row_recv, gsem_s, gsem_r, osem_s, osem_r, rsem_s, rsem_r,
):
    x = lax.axis_index("dp")
    n = lax.axis_index("expert")
    core = lax.rem(n, NC)
    z = lax.rem(n // NC, NZ)
    y = n // (NC * NZ)
    j = y * NC + core

    def expert_at(yy, zz, cc):
        return (yy * NZ + zz) * NC + cc

    def z_dev(d):
        return (x, expert_at(y, lax.rem(z + d, NZ), core))

    z_up, z_down = z_dev(1), z_dev(NZ - 1)
    x_up = (lax.rem(x + 1, NX), n)
    x_down = (lax.rem(x + NX - 1, NX), n)

    def flip(k):
        ky, kc = k // NC, k % NC
        if ky == 0:
            yy = y
        elif ky == 1:
            yy = y + 1 - 2 * lax.rem(y, 2)
        elif ky == 2:
            yy = lax.rem(y + 2, 4)
        else:
            yy = 3 - y
        cc = core if kc == 0 else 1 - core
        return yy, cc

    def group_dev(k):
        yy, cc = flip(k)
        return (x, expert_at(yy, z, cc))

    def group_pos(k):
        yy, cc = flip(k)
        return yy * NC + cc

    partners = [z_dev(d) for d in range(1, NZ)] + [x_up, x_down] + [group_dev(k) for k in range(1, GROUP)]

    def remote(src, dst, ssem, rsem, dev):
        return pltpu.make_async_remote_copy(
            src_ref=src, dst_ref=dst, send_sem=ssem, recv_sem=rsem,
            device_id=dev, device_id_type=pl.DeviceIdType.MESH,
        )

    barrier = pltpu.get_barrier_semaphore()
    for dev in partners:
        pl.semaphore_signal(barrier, inc=1, device_id=dev, device_id_type=pl.DeviceIdType.MESH)
    pending = []

    def start(copy):
        copy.start()
        pending.append(copy)
        return copy

    H = TOK // 2

    def token_copy(step, up, half):
        lo = half * H
        base = 0 if up else TOK
        if step == 1:
            src = grads_ref.at[pl.ds(lo, H)]
        else:
            src = tokens.at[step - 2, pl.ds(base + lo, H)]
        if step == HALF:
            dst = tokens.at[HALF - 1, pl.ds(TOK + lo, H)]
        else:
            dst = tokens.at[step - 1, pl.ds(base + lo, H)]
        d = 0 if up else 1
        return remote(
            src, dst, tok_send.at[d, step - 1, half], tok_recv.at[d, step - 1, half],
            z_up if up else z_down,
        )

    tok = {}
    for step in range(1, HALF):
        for half in range(2):
            for up in (True, False):
                tok[step, up, half] = token_copy(step, up, half)
    tok[HALF, True, 0] = token_copy(HALF, True, 0)
    tok[HALF, False, 1] = token_copy(HALF, False, 1)

    chosen = routes_ref[...]
    erow = iota((EXPERTS, TOK), 0)
    tcol = iota((EXPERTS, TOK), 1)
    onehot = jnp.zeros((EXPERTS, TOK), F32)
    for k in range(TOP):
        onehot += jnp.where(erow == chosen[k:k + 1, :], 1.0, 0.0)
    earlier = jnp.where(erow < tcol, 1.0, 0.0).astype(BF16)
    before = mm(onehot.astype(BF16), earlier)
    hot = jnp.sum(jnp.where(erow == tcol, jnp.broadcast_to(hot_ref[...].astype(F32), (EXPERTS, TOK)), 0.0),
                  axis=1, keepdims=True)
    limit = jnp.where(hot > 0.5, float(SLOTS), float(CAP))
    ranked = jnp.where(before < limit, before, 1000.0)
    zrow = iota((NZ, TOK), 0)
    irow = lax.rem(iota((TOK, TOK), 0), GROUP * SLOTS).astype(F32)
    token = (iota((NZ, TOK), 1) + 1).astype(F32)
    lefts, rights = [], []
    for k in range(TOP):
        e = chosen[k:k + 1, :]
        rank = jnp.sum(jnp.where(erow == e, ranked, 0.0), axis=0, keepdims=True)
        at = (((e // (NZ * NC)) * NC + lax.rem(e, NC)) * SLOTS).astype(F32) + rank
        here = zrow == lax.rem(e // NC, NZ)
        w = weight_ref[k:k + 1, :]
        w1 = w.astype(BF16).astype(F32)
        w2 = (w - w1).astype(BF16).astype(F32)
        w3 = w - w1 - w2
        lefts.append(jnp.concatenate(
            [jnp.where(here, v, 0.0) for v in (token, w1, w2, w3)], axis=0).astype(BF16))
        rights.append(jnp.where(irow == at, 1.0, 0.0).astype(BF16))
    found = lax.dot_general(jnp.concatenate(lefts, axis=1), jnp.concatenate(rights, axis=1),
                            (((1,), (1,)), ((), ())), preferred_element_type=F32)
    weights = found[NZ:2 * NZ] + found[2 * NZ:3 * NZ] + found[3 * NZ:4 * NZ]
    listing = jnp.where(iota((NZ, TOK), 1) < GROUP * SLOTS, found[0:NZ] - 1.0, weights)
    for zz in range(NZ):
        table[zz] = listing[zz:zz + 1, :]

    def table_copy(d):
        return remote(table.at[lax.rem(z + d, NZ)], table_in.at[z], tab_send.at[d], tab_recv.at[d], z_dev(d))

    pl.semaphore_wait(barrier, len(partners))
    for d in (1, 15, 2, 14, 3, 13, 4, 12, 5, 11, 6, 10, 7, 9, 8):
        start(table_copy(d))
    for half in range(2):
        for up in (True, False):
            start(tok[1, up, half])
    table_in[z] = table[z]

    def advance(step, half):
        for up in (True, False):
            if (step, up, half) in tok:
                tok[step, up, half].wait_recv()
                if (step + 1, up, half) in tok:
                    start(tok[step + 1, up, half])

    ri = iota((GROUP * 2 * SLOTS, TOK), 0)
    rl = iota((GROUP * 2 * SLOTS, TOK), 1)
    from_l = lax.rem(ri // SLOTS, 2) == 0
    rslot = (ri // (2 * SLOTS)) * SLOTS + lax.rem(ri, SLOTS)
    at_token = rl == rslot
    at_weight = rl == rslot + GROUP * SLOTS
    lane = rl.astype(F32)

    def dispatch(pair):
        if pair == HALF - 1:
            t_l, t_r = table_in[z], table_in[lax.rem(z + HALF, NZ)]
            g_l = grads_ref[...]
        else:
            t_l, t_r = table_in[lax.rem(z + NZ - 1 - pair, NZ)], table_in[lax.rem(z + 1 + pair, NZ)]
            g_l = tokens[pair, 0:TOK]
        g_r = tokens[pair, TOK:2 * TOK]
        both = jnp.where(from_l, t_l, t_r)
        token_of = jnp.sum(jnp.where(at_token, both, 0.0), axis=1, keepdims=True)
        weight = jnp.sum(jnp.where(at_weight, both, 0.0), axis=1, keepdims=True)
        hit = jnp.where(lane == token_of, 1.0, 0.0)
        s_l = jnp.where(from_l, hit, 0.0).astype(BF16)
        s_r = jnp.where(from_l, 0.0, hit).astype(BF16)
        rows = ((mm(s_l, g_l) + mm(s_r, g_r)) * weight).astype(BF16)
        rows_out[pair] = rows.reshape(GROUP, 2 * SLOTS, WIDTH)
        for k in (4, 5, 2, 3, 6, 7, 1):
            start(row_copy(pair, k))
        rows_in[pair, 0] = rows_out[pair, j]

    def row_copy(pair, k):
        return remote(rows_out.at[pair, group_pos(k)], rows_in.at[pair, k],
                      row_send.at[pair, k], row_recv.at[pair, k], group_dev(k))

    def send_counts():
        for d in range(1, NZ):
            table_copy(d).wait_recv()
        used = jnp.where(table_in[...].reshape(NZ, TOK) >= 0.0, 1.0, 0.0).astype(BF16)
        src = iota((TOK, TOK), 0)
        hosted = iota((TOK, TOK), 1) >= TOK // 2
        for jj in range(GROUP):
            want = jnp.where(hosted, jj ^ (GROUP // 2), jj)
            counts[jj] = mm(used, jnp.where(src // SLOTS == want, 1.0, 0.0).astype(BF16))
        for k in range(1, GROUP):
            start(cnt_copy(k))
        counts_in[j] = counts[j]

    def cnt_copy(k):
        return remote(counts.at[group_pos(k)], counts_in.at[j], cnt_send.at[k], cnt_recv.at[k], group_dev(k))

    def masks():
        for k in range(1, GROUP):
            cnt_copy(k).wait_recv()
        per = counts_in[...].reshape(EXPERTS, TOK).astype(BF16)
        rr = EXPERTS * SLOTS
        source = iota((rr, EXPERTS), 0) // SLOTS
        m = iota((rr, EXPERTS), 1)
        place = ((m // (NC * NZ)) * NZ + lax.rem(m, NZ)) * NC + lax.rem(m // NZ, NC)
        spread = jnp.where(source == place, 1.0, 0.0).astype(BF16)
        each = mm(spread, per).astype(BF16)
        slot = lax.rem(iota((rr, TOK), 0), SLOTS)
        for i in range(2):
            pickone = jnp.where(iota((TOK, TOK), 0) == i * (TOK // 2), 1.0, 0.0).astype(BF16)
            many = mm(each, pickone)
            good = (many > slot.astype(F32)) & ((slot >= CAP) if i else (slot < CAP))
            keep[i] = jnp.where(good, 1.0, 0.0).astype(BF16)

    def input_gram(gram, which, i):
        block = 256
        cols = pl.ds(i * block, block)
        kept = jnp.concatenate([keep[which]] * (block // TOK), axis=1)
        gram[cols, :] = lax.dot_general(
            inputs_ref[:, cols] * kept, inputs_ref[...], TN, preferred_element_type=F32)

    class Scatter:
        def __init__(self, gram, rows, out, via, l_in, r_in, ssem, rsem):
            self.gram, self.rows, self.out, self.via = gram, rows, out, via
            self.l_in, self.r_in, self.ssem, self.rsem = l_in, r_in, ssem, rsem
            self.h = rows // 2

        def part(self, blk, half):
            at = pl.multiple_of(blk * self.rows + half * self.h, 32)
            return self.gram[pl.ds(at, self.h), :]

        def copies(self):
            h = self.h
            lo, hi = pl.ds(0, h), pl.ds(h, h)
            ends = [
                (self.via.at[0], x_up), (self.via.at[1], x_down),
                (self.l_in.at[hi], x_up), (self.r_in.at[lo], x_down),
                (self.l_in.at[lo], x_up), (self.r_in.at[hi], x_down),
            ]
            return [remote(self.out.at[i], dst, self.ssem.at[i], self.rsem.at[i], dev)
                    for i, (dst, dev) in enumerate(ends)]

        def first(self, ready=None):
            self.c = self.copies()
            opposite = lax.rem(x + 2, NX)
            nxt, prv = lax.rem(x + 1, NX), lax.rem(x + NX - 1, NX)
            if ready is not None:
                ready(opposite)
            self.out[0] = self.part(opposite, 0).astype(BF16)
            start(self.c[0])
            self.out[1] = self.part(opposite, 1).astype(BF16)
            start(self.c[1])
            if ready is not None:
                ready(nxt)
            self.out[2] = self.part(nxt, 1).astype(BF16)
            start(self.c[2])
            if ready is not None:
                ready(prv)
            self.out[3] = self.part(prv, 0).astype(BF16)
            start(self.c[3])
            if ready is not None:
                ready(x)

        def second(self):
            nxt, prv = lax.rem(x + 1, NX), lax.rem(x + NX - 1, NX)
            self.c[0].wait_recv()
            self.out[4] = (self.part(nxt, 0) + self.via[0].astype(F32)).astype(BF16)
            start(self.c[4])
            self.c[1].wait_recv()
            self.out[5] = (self.part(prv, 1) + self.via[1].astype(F32)).astype(BF16)
            start(self.c[5])

        def last(self, put):
            h = self.h
            lo, hi = pl.ds(0, h), pl.ds(h, h)
            self.c[2].wait_recv()
            self.c[3].wait_recv()
            self.c[4].wait_recv()
            put(lo, self.part(x, 0) + self.l_in[lo].astype(F32) + self.r_in[lo].astype(F32))
            self.c[5].wait_recv()
            put(hi, self.part(x, 1) + self.l_in[hi].astype(F32) + self.r_in[hi].astype(F32))

    factor = 1.0 / (TOK * TOP * NX)

    own = Scatter(gram_o, HIDDEN // NX, os_out, os_via, os_l, os_r, osem_s, osem_r)
    rep = Scatter(gram_r, HIDDEN // NX, rs_out, rs_via, rs_l, rs_r, rsem_s, rsem_r)
    gs = Scatter(gram_g, WIDTH // NX, gs_out, gs_via, gs_l, gs_r, gsem_s, gsem_r)

    def rows_ready(first_pair, pairs):
        for p in range(first_pair, first_pair + pairs):
            for k in range(1, GROUP):
                row_copy(p, k).wait_recv()

    def gram_rows(first_pair, pairs, blk, fresh):
        kk = pairs * GROUP * 2 * SLOTS
        at = pl.multiple_of(blk * 256, 256)
        a = rows_in[first_pair:first_pair + pairs, :, :, pl.ds(at, 256)].reshape(kk, 256)
        b = rows_in[first_pair:first_pair + pairs].reshape(kk, WIDTH)
        r = lax.dot_general(a, b, TN, preferred_element_type=F32)
        if fresh:
            gram_g[pl.ds(at, 256), :] = r
        else:
            gram_g[pl.ds(at, 256), :] += r

    def gram_part(first_pair, pairs, fresh):
        rows_ready(first_pair, pairs)

        def body(i, carry):
            gram_rows(first_pair, pairs, i, fresh)
            return carry

        lax.fori_loop(0, WIDTH // 256, body, 0)

    far = remote(mine, theirs, far_sem.at[0], far_sem.at[1], group_dev(4))

    def put_mine(at, value):
        mine[at, :] = value.astype(BF16)

    def put_input(at, value):
        input_out[at, :] = (value + theirs[at, :].astype(F32)) * factor

    def put_grad(at, value):
        grad_out[at, :] = value * factor

    advance(1, 0)
    send_counts()
    advance(1, 1)
    dispatch(0)
    advance(2, 0)
    masks()
    input_gram(gram_r, 1, 0)
    advance(2, 1)
    dispatch(1)
    input_gram(gram_r, 1, 1)
    advance(3, 0)
    input_gram(gram_r, 1, 2)
    rep.first()
    advance(3, 1)
    dispatch(2)
    input_gram(gram_o, 0, 0)
    advance(4, 0)
    input_gram(gram_o, 0, 1)
    input_gram(gram_o, 0, 2)
    advance(4, 1)
    dispatch(3)
    rep.second()
    advance(5, 0)
    own.first()
    rep.last(put_mine)
    start(far)
    advance(5, 1)
    dispatch(4)
    advance(6, 0)
    gram_part(0, 2, True)
    advance(6, 1)
    dispatch(5)
    own.second()
    advance(7, 0)
    gram_part(2, 2, False)
    advance(7, 1)
    dispatch(6)
    gram_part(4, 2, False)
    far.wait_recv()
    own.last(put_input)
    advance(8, 0)
    advance(8, 1)
    dispatch(7)
    rows_ready(6, 2)
    gs.first(lambda blk: gram_rows(6, 2, blk, False))
    gs.second()
    gs.last(put_grad)
    for copy in pending:
        copy.wait_send()


def shards(grads, route_weight, routes, hot, expert_inputs):
    inputs = expert_inputs.reshape(EXPERTS * SLOTS, HIDDEN)
    vmem = pl.BlockSpec(memory_space=pltpu.VMEM)
    dma = pltpu.SemaphoreType.DMA
    hg, hx = WIDTH // NX // 2, HIDDEN // NX // 2
    grad_rows, input_rows = pl.pallas_call(
        kernel,
        out_shape=(
            jax.ShapeDtypeStruct((WIDTH // NX, WIDTH), F32),
            jax.ShapeDtypeStruct((HIDDEN // NX, HIDDEN), F32),
        ),
        in_specs=[vmem] * 5,
        out_specs=(vmem, vmem),
        scratch_shapes=[
            pltpu.VMEM((HALF, 2 * TOK, WIDTH), BF16),
            pltpu.VMEM((NZ, 1, TOK), F32),
            pltpu.VMEM((NZ, 1, TOK), F32),
            pltpu.VMEM((2, EXPERTS * SLOTS, TOK), BF16),
            pltpu.VMEM((GROUP, NZ, TOK), F32),
            pltpu.VMEM((GROUP, NZ, TOK), F32),
            pltpu.VMEM((HALF, GROUP, 2 * SLOTS, WIDTH), BF16),
            pltpu.VMEM((HALF, GROUP, 2 * SLOTS, WIDTH), BF16),
            pltpu.VMEM((WIDTH, WIDTH), F32),
            pltpu.VMEM((HIDDEN, HIDDEN), F32),
            pltpu.VMEM((HIDDEN, HIDDEN), F32),
            pltpu.VMEM((2 * hx, HIDDEN), BF16),
            pltpu.VMEM((2 * hx, HIDDEN), BF16),
            pltpu.VMEM((6, hg, WIDTH), BF16),
            pltpu.VMEM((2, hg, WIDTH), BF16),
            pltpu.VMEM((2 * hg, WIDTH), BF16),
            pltpu.VMEM((2 * hg, WIDTH), BF16),
            pltpu.VMEM((6, hx, HIDDEN), BF16),
            pltpu.VMEM((2, hx, HIDDEN), BF16),
            pltpu.VMEM((2 * hx, HIDDEN), BF16),
            pltpu.VMEM((2 * hx, HIDDEN), BF16),
            pltpu.VMEM((6, hx, HIDDEN), BF16),
            pltpu.VMEM((2, hx, HIDDEN), BF16),
            pltpu.VMEM((2 * hx, HIDDEN), BF16),
            pltpu.VMEM((2 * hx, HIDDEN), BF16),
            dma((2, HALF, 2)), dma((2, HALF, 2)),
            dma((NZ,)), dma((NZ,)),
            dma((2,)),
            dma((GROUP,)), dma((GROUP,)),
            dma((HALF, GROUP)), dma((HALF, GROUP)),
            dma((6,)), dma((6,)), dma((6,)), dma((6,)), dma((6,)), dma((6,)),
        ],
        compiler_params=pltpu.CompilerParams(
            collective_id=0, has_side_effects=True, vmem_limit_bytes=48 * 1024 * 1024
        ),
    )(routes.T, route_weight.T, hot.reshape(1, EXPERTS), grads, inputs)
    return input_rows[:, None, :], grad_rows[:, None, :]


def solution(mesh):
    return jax.shard_map(
        shards,
        mesh=mesh,
        in_specs=(
            P(("dp", "expert"), None),
            P(("dp", "expert"), None),
            P(("dp", "expert"), None),
            P(),
            P("dp", "expert", None, None, None, None, None),
        ),
        out_specs=(P("dp", "expert", None), P("dp", "expert", None)),
        check_vma=False,
    )
```

```python
import jax
import jax.numpy as jnp
from jax import lax
from jax.experimental import pallas as pl
from jax.experimental.pallas import tpu as pltpu
from jax.sharding import PartitionSpec as P

NY, NZ, NC, NX = 4, 16, 2, 4
GROUP = NY * NC
HALF = NZ // 2
TOK, TOP, EXPERTS, CAP = 128, 8, 128, 4
WIDTH, HIDDEN = 1024, 768
SLOTS = 2 * CAP
F32, BF16 = jnp.float32, jnp.bfloat16
TN = (((0,), (0,)), ((), ()))


def mm(a, b):
    return jnp.dot(a, b, preferred_element_type=F32)


def iota(shape, dim):
    return lax.broadcasted_iota(jnp.int32, shape, dim)


def kernel(
    routes_hbm, weight_hbm, hot_hbm, grads_hbm, inputs_hbm,
    grad_hbm, input_hbm,
    routes_ref, weight_ref, hot_ref, grads_ref, grad_out, input_out, out_sem, inputs_raw, inputs_ref, in_sem, tokens, table, table_in, keep, counts, counts_in,
    rows_out, rows_in, gram_g, gram_o, gram_r, mine, theirs,
    gs_out, gs_via, gs_l, gs_r, os_out, os_via, os_l, os_r, rs_out, rs_via, rs_l, rs_r,
    tok_send, tok_recv, tab_send, tab_recv, far_sem, cnt_send, cnt_recv,
    row_send, row_recv, gsem_s, gsem_r, osem_s, osem_r, rsem_s, rsem_r,
):
    x = lax.axis_index("dp")
    n = lax.axis_index("expert")
    core = lax.rem(n, NC)
    z = lax.rem(n // NC, NZ)
    y = n // (NC * NZ)
    j = y * NC + core

    def expert_at(yy, zz, cc):
        return (yy * NZ + zz) * NC + cc

    def z_dev(d):
        return (x, expert_at(y, lax.rem(z + d, NZ), core))

    z_up, z_down = z_dev(1), z_dev(NZ - 1)
    x_up = (lax.rem(x + 1, NX), n)
    x_down = (lax.rem(x + NX - 1, NX), n)

    def flip(k):
        ky, kc = k // NC, k % NC
        if ky == 0:
            yy = y
        elif ky == 1:
            yy = y + 1 - 2 * lax.rem(y, 2)
        elif ky == 2:
            yy = lax.rem(y + 2, 4)
        else:
            yy = 3 - y
        cc = core if kc == 0 else 1 - core
        return yy, cc

    def group_dev(k):
        yy, cc = flip(k)
        return (x, expert_at(yy, z, cc))

    def group_pos(k):
        yy, cc = flip(k)
        return yy * NC + cc

    partners = [z_dev(d) for d in range(1, NZ)] + [x_up, x_down] + [group_dev(k) for k in range(1, GROUP)]

    def remote(src, dst, ssem, rsem, dev):
        return pltpu.make_async_remote_copy(
            src_ref=src, dst_ref=dst, send_sem=ssem, recv_sem=rsem,
            device_id=dev, device_id_type=pl.DeviceIdType.MESH,
        )

    loads = [
        pltpu.make_async_copy(a, b, in_sem.at[i])
        for i, (a, b) in enumerate([
            (grads_hbm, grads_ref), (routes_hbm, routes_ref), (weight_hbm, weight_ref), (hot_hbm, hot_ref),
            (inputs_hbm, inputs_raw),
        ])
    ]
    for load in loads:
        load.start()
    barrier = pltpu.get_barrier_semaphore()
    for dev in partners:
        pl.semaphore_signal(barrier, inc=1, device_id=dev, device_id_type=pl.DeviceIdType.MESH)
    pending = []

    def start(copy):
        copy.start()
        pending.append(copy)
        return copy

    H = TOK // 2

    def token_copy(step, up, half):
        lo = half * H
        base = 0 if up else TOK
        if step == 1:
            src = grads_ref.at[pl.ds(lo, H)]
        else:
            src = tokens.at[step - 2, pl.ds(base + lo, H)]
        if step == HALF:
            dst = tokens.at[HALF - 1, pl.ds(TOK + lo, H)]
        else:
            dst = tokens.at[step - 1, pl.ds(base + lo, H)]
        d = 0 if up else 1
        return remote(
            src, dst, tok_send.at[d, step - 1, half], tok_recv.at[d, step - 1, half],
            z_up if up else z_down,
        )

    tok = {}
    for step in range(1, HALF):
        for half in range(2):
            for up in (True, False):
                tok[step, up, half] = token_copy(step, up, half)
    tok[HALF, True, 0] = token_copy(HALF, True, 0)
    tok[HALF, False, 1] = token_copy(HALF, False, 1)

    for load in loads[1:4]:
        load.wait()

    chosen = routes_ref[...]
    erow = iota((EXPERTS, TOK), 0)
    tcol = iota((EXPERTS, TOK), 1)
    onehot = jnp.zeros((EXPERTS, TOK), F32)
    for k in range(TOP):
        onehot += jnp.where(erow == chosen[k:k + 1, :], 1.0, 0.0)
    earlier = jnp.where(erow < tcol, 1.0, 0.0).astype(BF16)
    before = mm(onehot.astype(BF16), earlier)
    hot = jnp.sum(jnp.where(erow == tcol, jnp.broadcast_to(hot_ref[...].astype(F32), (EXPERTS, TOK)), 0.0),
                  axis=1, keepdims=True)
    limit = jnp.where(hot > 0.5, float(SLOTS), float(CAP))
    ranked = jnp.where(before < limit, before, 1000.0)
    zrow = iota((NZ, TOK), 0)
    irow = lax.rem(iota((TOK, TOK), 0), GROUP * SLOTS).astype(F32)
    token = (iota((NZ, TOK), 1) + 1).astype(F32)
    lefts, rights = [], []
    for k in range(TOP):
        e = chosen[k:k + 1, :]
        rank = jnp.sum(jnp.where(erow == e, ranked, 0.0), axis=0, keepdims=True)
        at = (((e // (NZ * NC)) * NC + lax.rem(e, NC)) * SLOTS).astype(F32) + rank
        here = zrow == lax.rem(e // NC, NZ)
        w = weight_ref[k:k + 1, :]
        w1 = w.astype(BF16).astype(F32)
        w2 = (w - w1).astype(BF16).astype(F32)
        w3 = w - w1 - w2
        lefts.append(jnp.concatenate(
            [jnp.where(here, v, 0.0) for v in (token, w1, w2, w3)], axis=0).astype(BF16))
        rights.append(jnp.where(irow == at, 1.0, 0.0).astype(BF16))
    found = lax.dot_general(jnp.concatenate(lefts, axis=1), jnp.concatenate(rights, axis=1),
                            (((1,), (1,)), ((), ())), preferred_element_type=F32)
    weights = found[NZ:2 * NZ] + found[2 * NZ:3 * NZ] + found[3 * NZ:4 * NZ]
    listing = jnp.where(iota((NZ, TOK), 1) < GROUP * SLOTS, found[0:NZ] - 1.0, weights)
    for zz in range(NZ):
        table[zz] = listing[zz:zz + 1, :]

    def table_copy(d):
        return remote(table.at[lax.rem(z + d, NZ)], table_in.at[z], tab_send.at[d], tab_recv.at[d], z_dev(d))

    pl.semaphore_wait(barrier, len(partners))
    for d in (1, 15, 2, 14, 3, 13, 4, 12, 5, 11, 6, 10, 7, 9, 8):
        start(table_copy(d))
    loads[0].wait()
    for half in range(2):
        for up in (True, False):
            start(tok[1, up, half])
    table_in[z] = table[z]

    def advance(step, half):
        for up in (True, False):
            if (step, up, half) in tok:
                tok[step, up, half].wait_recv()
                if (step + 1, up, half) in tok:
                    start(tok[step + 1, up, half])

    ri = iota((GROUP * 2 * SLOTS, TOK), 0)
    rl = iota((GROUP * 2 * SLOTS, TOK), 1)
    from_l = lax.rem(ri // SLOTS, 2) == 0
    rslot = (ri // (2 * SLOTS)) * SLOTS + lax.rem(ri, SLOTS)
    at_token = rl == rslot
    at_weight = rl == rslot + GROUP * SLOTS
    lane = rl.astype(F32)

    def dispatch(pair):
        if pair == HALF - 1:
            t_l, t_r = table_in[z], table_in[lax.rem(z + HALF, NZ)]
            g_l = grads_ref[...]
        else:
            t_l, t_r = table_in[lax.rem(z + NZ - 1 - pair, NZ)], table_in[lax.rem(z + 1 + pair, NZ)]
            g_l = tokens[pair, 0:TOK]
        g_r = tokens[pair, TOK:2 * TOK]
        both = jnp.where(from_l, t_l, t_r)
        token_of = jnp.sum(jnp.where(at_token, both, 0.0), axis=1, keepdims=True)
        weight = jnp.sum(jnp.where(at_weight, both, 0.0), axis=1, keepdims=True)
        hit = jnp.where(lane == token_of, 1.0, 0.0)
        s_l = jnp.where(from_l, hit, 0.0).astype(BF16)
        s_r = jnp.where(from_l, 0.0, hit).astype(BF16)
        rows = ((mm(s_l, g_l) + mm(s_r, g_r)) * weight).astype(BF16)
        rows_out[pair] = rows.reshape(GROUP, 2 * SLOTS, WIDTH)
        for k in (4, 5, 2, 3, 6, 7, 1):
            start(row_copy(pair, k))
        rows_in[pair, 0] = rows_out[pair, j]

    def row_copy(pair, k):
        return remote(rows_out.at[pair, group_pos(k)], rows_in.at[pair, k],
                      row_send.at[pair, k], row_recv.at[pair, k], group_dev(k))

    def send_counts():
        for d in range(1, NZ):
            table_copy(d).wait_recv()
        used = jnp.where(table_in[...].reshape(NZ, TOK) >= 0.0, 1.0, 0.0).astype(BF16)
        src = iota((TOK, TOK), 0)
        hosted = iota((TOK, TOK), 1) >= TOK // 2
        for jj in range(GROUP):
            want = jnp.where(hosted, jj ^ (GROUP // 2), jj)
            counts[jj] = mm(used, jnp.where(src // SLOTS == want, 1.0, 0.0).astype(BF16))
        for k in range(1, GROUP):
            start(cnt_copy(k))
        counts_in[j] = counts[j]

    def cnt_copy(k):
        return remote(counts.at[group_pos(k)], counts_in.at[j], cnt_send.at[k], cnt_recv.at[k], group_dev(k))

    def masks():
        for k in range(1, GROUP):
            cnt_copy(k).wait_recv()
        per = counts_in[...].reshape(EXPERTS, TOK).astype(BF16)
        rr = EXPERTS * SLOTS
        source = iota((rr, EXPERTS), 0) // SLOTS
        m = iota((rr, EXPERTS), 1)
        place = ((m // (NC * NZ)) * NZ + lax.rem(m, NZ)) * NC + lax.rem(m // NZ, NC)
        spread = jnp.where(source == place, 1.0, 0.0).astype(BF16)
        each = mm(spread, per).astype(BF16)
        slot = lax.rem(iota((rr, TOK), 0), SLOTS)
        for i in range(2):
            pickone = jnp.where(iota((TOK, TOK), 0) == i * (TOK // 2), 1.0, 0.0).astype(BF16)
            many = mm(each, pickone)
            good = (many > slot.astype(F32)) & ((slot >= CAP) if i else (slot < CAP))
            keep[i] = jnp.where(good, 1.0, 0.0).astype(BF16)

    def unfold(part):
        step = 8
        count = EXPERTS // step

        def body(i, carry):
            at = pl.multiple_of(i * step * CAP, step * CAP)
            inputs_ref[pl.ds(at, step * CAP), :] = inputs_raw[pl.ds(i * step, step)].reshape(step * CAP, HIDDEN)
            return carry

        lax.fori_loop(part * count, (part + 1) * count, body, 0)

    def input_gram(gram, which, i):
        block = 256
        cols = pl.ds(i * block, block)
        kept = jnp.concatenate([keep[which]] * (block // TOK), axis=1)
        gram[cols, :] = lax.dot_general(
            inputs_ref[:, cols] * kept, inputs_ref[...], TN, preferred_element_type=F32)

    class Scatter:
        def __init__(self, gram, rows, out, via, l_in, r_in, ssem, rsem):
            self.gram, self.rows, self.out, self.via = gram, rows, out, via
            self.l_in, self.r_in, self.ssem, self.rsem = l_in, r_in, ssem, rsem
            self.h = rows // 2

        def part(self, blk, half):
            at = pl.multiple_of(blk * self.rows + half * self.h, 32)
            return self.gram[pl.ds(at, self.h), :]

        def copies(self):
            h = self.h
            lo, hi = pl.ds(0, h), pl.ds(h, h)
            ends = [
                (self.via.at[0], x_up), (self.via.at[1], x_down),
                (self.l_in.at[hi], x_up), (self.r_in.at[lo], x_down),
                (self.l_in.at[lo], x_up), (self.r_in.at[hi], x_down),
            ]
            return [remote(self.out.at[i], dst, self.ssem.at[i], self.rsem.at[i], dev)
                    for i, (dst, dev) in enumerate(ends)]

        def first(self, ready=None):
            self.c = self.copies()
            opposite = lax.rem(x + 2, NX)
            nxt, prv = lax.rem(x + 1, NX), lax.rem(x + NX - 1, NX)
            if ready is not None:
                ready(opposite)
            self.out[0] = self.part(opposite, 0).astype(BF16)
            start(self.c[0])
            self.out[1] = self.part(opposite, 1).astype(BF16)
            start(self.c[1])
            if ready is not None:
                ready(nxt)
            self.out[2] = self.part(nxt, 1).astype(BF16)
            start(self.c[2])
            if ready is not None:
                ready(prv)
            self.out[3] = self.part(prv, 0).astype(BF16)
            start(self.c[3])
            if ready is not None:
                ready(x)

        def second(self):
            nxt, prv = lax.rem(x + 1, NX), lax.rem(x + NX - 1, NX)
            self.c[0].wait_recv()
            self.out[4] = (self.part(nxt, 0) + self.via[0].astype(F32)).astype(BF16)
            start(self.c[4])
            self.c[1].wait_recv()
            self.out[5] = (self.part(prv, 1) + self.via[1].astype(F32)).astype(BF16)
            start(self.c[5])

        def last(self, put):
            h = self.h
            lo, hi = pl.ds(0, h), pl.ds(h, h)
            self.c[2].wait_recv()
            self.c[3].wait_recv()
            self.c[4].wait_recv()
            put(lo, self.part(x, 0) + self.l_in[lo].astype(F32) + self.r_in[lo].astype(F32))
            self.c[5].wait_recv()
            put(hi, self.part(x, 1) + self.l_in[hi].astype(F32) + self.r_in[hi].astype(F32))

    factor = 1.0 / (TOK * TOP * NX)

    own = Scatter(gram_o, HIDDEN // NX, os_out, os_via, os_l, os_r, osem_s, osem_r)
    rep = Scatter(gram_r, HIDDEN // NX, rs_out, rs_via, rs_l, rs_r, rsem_s, rsem_r)
    gs = Scatter(gram_g, WIDTH // NX, gs_out, gs_via, gs_l, gs_r, gsem_s, gsem_r)

    def rows_ready(first_pair, pairs):
        for p in range(first_pair, first_pair + pairs):
            for k in range(1, GROUP):
                row_copy(p, k).wait_recv()

    def gram_rows(first_pair, pairs, blk, fresh):
        kk = pairs * GROUP * 2 * SLOTS
        at = pl.multiple_of(blk * 256, 256)
        a = rows_in[first_pair:first_pair + pairs, :, :, pl.ds(at, 256)].reshape(kk, 256)
        b = rows_in[first_pair:first_pair + pairs].reshape(kk, WIDTH)
        r = lax.dot_general(a, b, TN, preferred_element_type=F32)
        if fresh:
            gram_g[pl.ds(at, 256), :] = r
        else:
            gram_g[pl.ds(at, 256), :] += r

    def gram_part(first_pair, pairs, fresh):
        rows_ready(first_pair, pairs)

        def body(i, carry):
            gram_rows(first_pair, pairs, i, fresh)
            return carry

        lax.fori_loop(0, WIDTH // 256, body, 0)

    far = remote(mine, theirs, far_sem.at[0], far_sem.at[1], group_dev(4))

    saves = []

    def save(src, dst, at, first):
        copy = pltpu.make_async_copy(src.at[at], dst.at[at, 0], out_sem.at[first + (1 if at.start else 0)])
        copy.start()
        saves.append(copy)

    def put_mine(at, value):
        mine[at, :] = value.astype(BF16)

    def put_input(at, value):
        input_out[at, :] = (value + theirs[at, :].astype(F32)) * factor
        save(input_out, input_hbm, at, 0)

    def put_grad(at, value):
        grad_out[at, :] = value * factor
        save(grad_out, grad_hbm, at, 2)

    loads[4].wait()
    advance(1, 0)
    send_counts()
    advance(1, 1)
    dispatch(0)
    advance(2, 0)
    masks()
    unfold(0)
    advance(2, 1)
    dispatch(1)
    unfold(1)
    advance(3, 0)
    input_gram(gram_r, 1, 0)
    input_gram(gram_r, 1, 1)
    input_gram(gram_r, 1, 2)
    rep.first()
    advance(3, 1)
    dispatch(2)
    input_gram(gram_o, 0, 0)
    advance(4, 0)
    input_gram(gram_o, 0, 1)
    input_gram(gram_o, 0, 2)
    advance(4, 1)
    dispatch(3)
    rep.second()
    advance(5, 0)
    own.first()
    rep.last(put_mine)
    start(far)
    advance(5, 1)
    dispatch(4)
    advance(6, 0)
    gram_part(0, 2, True)
    advance(6, 1)
    dispatch(5)
    own.second()
    advance(7, 0)
    gram_part(2, 2, False)
    advance(7, 1)
    dispatch(6)
    gram_part(4, 2, False)
    far.wait_recv()
    own.last(put_input)
    advance(8, 0)
    advance(8, 1)
    dispatch(7)
    rows_ready(6, 2)
    gs.first(lambda blk: gram_rows(6, 2, blk, False))
    gs.second()
    gs.last(put_grad)
    for copy in pending:
        copy.wait_send()
    for copy in saves:
        copy.wait()


def shards(grads, route_weight, routes, hot, expert_inputs):
    inputs = expert_inputs.reshape(EXPERTS * 2, CAP, HIDDEN)
    hbm = pl.BlockSpec(memory_space=pl.ANY)
    dma = pltpu.SemaphoreType.DMA
    hg, hx = WIDTH // NX // 2, HIDDEN // NX // 2
    grad_factor, input_factor = pl.pallas_call(
        kernel,
        out_shape=(
            jax.ShapeDtypeStruct((WIDTH // NX, 1, WIDTH), F32),
            jax.ShapeDtypeStruct((HIDDEN // NX, 1, HIDDEN), F32),
        ),
        in_specs=[hbm] * 5,
        out_specs=(hbm, hbm),
        scratch_shapes=[
            pltpu.VMEM((TOP, TOK), jnp.int32),
            pltpu.VMEM((TOP, TOK), F32),
            pltpu.VMEM((1, EXPERTS), jnp.int32),
            pltpu.VMEM((TOK, WIDTH), BF16),
            pltpu.VMEM((WIDTH // NX, WIDTH), F32),
            pltpu.VMEM((HIDDEN // NX, HIDDEN), F32),
            dma((4,)),
            pltpu.VMEM((EXPERTS * 2, CAP, HIDDEN), BF16),
            pltpu.VMEM((EXPERTS * SLOTS, HIDDEN), BF16),
            dma((5,)),
            pltpu.VMEM((HALF, 2 * TOK, WIDTH), BF16),
            pltpu.VMEM((NZ, 1, TOK), F32),
            pltpu.VMEM((NZ, 1, TOK), F32),
            pltpu.VMEM((2, EXPERTS * SLOTS, TOK), BF16),
            pltpu.VMEM((GROUP, NZ, TOK), F32),
            pltpu.VMEM((GROUP, NZ, TOK), F32),
            pltpu.VMEM((HALF, GROUP, 2 * SLOTS, WIDTH), BF16),
            pltpu.VMEM((HALF, GROUP, 2 * SLOTS, WIDTH), BF16),
            pltpu.VMEM((WIDTH, WIDTH), F32),
            pltpu.VMEM((HIDDEN, HIDDEN), F32),
            pltpu.VMEM((HIDDEN, HIDDEN), F32),
            pltpu.VMEM((2 * hx, HIDDEN), BF16),
            pltpu.VMEM((2 * hx, HIDDEN), BF16),
            pltpu.VMEM((6, hg, WIDTH), BF16),
            pltpu.VMEM((2, hg, WIDTH), BF16),
            pltpu.VMEM((2 * hg, WIDTH), BF16),
            pltpu.VMEM((2 * hg, WIDTH), BF16),
            pltpu.VMEM((6, hx, HIDDEN), BF16),
            pltpu.VMEM((2, hx, HIDDEN), BF16),
            pltpu.VMEM((2 * hx, HIDDEN), BF16),
            pltpu.VMEM((2 * hx, HIDDEN), BF16),
            pltpu.VMEM((6, hx, HIDDEN), BF16),
            pltpu.VMEM((2, hx, HIDDEN), BF16),
            pltpu.VMEM((2 * hx, HIDDEN), BF16),
            pltpu.VMEM((2 * hx, HIDDEN), BF16),
            dma((2, HALF, 2)), dma((2, HALF, 2)),
            dma((NZ,)), dma((NZ,)),
            dma((2,)),
            dma((GROUP,)), dma((GROUP,)),
            dma((HALF, GROUP)), dma((HALF, GROUP)),
            dma((6,)), dma((6,)), dma((6,)), dma((6,)), dma((6,)), dma((6,)),
        ],
        compiler_params=pltpu.CompilerParams(
            collective_id=0, has_side_effects=True, vmem_limit_bytes=60 * 1024 * 1024
        ),
    )(routes.T, route_weight.T, hot.reshape(1, EXPERTS), grads, inputs)
    return input_factor, grad_factor


def solution(mesh):
    return jax.shard_map(
        shards,
        mesh=mesh,
        in_specs=(
            P(("dp", "expert"), None),
            P(("dp", "expert"), None),
            P(("dp", "expert"), None),
            P(),
            P("dp", "expert", None, None, None, None, None),
        ),
        out_specs=(P("dp", "expert", None), P("dp", "expert", None)),
        check_vma=False,
    )
```

```python
import jax
import jax.numpy as jnp
from jax import lax
from jax.experimental import pallas as pl
from jax.experimental.pallas import tpu as pltpu
from jax.sharding import PartitionSpec as P

NY, NZ, NC, NX = 4, 16, 2, 4
GROUP = NY * NC
HALF = NZ // 2
TOK, TOP, EXPERTS, CAP = 128, 8, 128, 4
WIDTH, HIDDEN = 1024, 768
SLOTS = 2 * CAP
F32, BF16 = jnp.float32, jnp.bfloat16
TN = (((0,), (0,)), ((), ()))


def mm(a, b):
    return jnp.dot(a, b, preferred_element_type=F32)


def iota(shape, dim):
    return lax.broadcasted_iota(jnp.int32, shape, dim)


def kernel(
    routes_hbm, weight_hbm, hot_hbm, grads_hbm, inputs_hbm,
    grad_hbm, input_hbm,
    routes_ref, weight_ref, hot_ref, grads_ref, grad_out, input_out, out_sem, inputs_raw, inputs_ref, in_sem, tokens, table, table_in, keep, counts, counts_in,
    rows_out, rows_in, fold_out, fold_in, fold_send, fold_recv, gram_g, gram_o, gram_r, mine, theirs,
    gs_out, gs_via, gs_l, gs_r, os_out, os_via, os_l, os_r, rs_out, rs_via, rs_l, rs_r,
    tok_send, tok_recv, tab_send, tab_recv, far_sem, cnt_send, cnt_recv,
    row_send, row_recv, gsem_s, gsem_r, osem_s, osem_r, rsem_s, rsem_r,
):
    x = lax.axis_index("dp")
    n = lax.axis_index("expert")
    core = lax.rem(n, NC)
    z = lax.rem(n // NC, NZ)
    y = n // (NC * NZ)
    j = y * NC + core

    def expert_at(yy, zz, cc):
        return (yy * NZ + zz) * NC + cc

    def z_dev(d):
        return (x, expert_at(y, lax.rem(z + d, NZ), core))

    z_up, z_down = z_dev(1), z_dev(NZ - 1)
    x_up = (lax.rem(x + 1, NX), n)
    x_down = (lax.rem(x + NX - 1, NX), n)

    def flip(k):
        ky, kc = k // NC, k % NC
        if ky == 0:
            yy = y
        elif ky == 1:
            yy = y + 1 - 2 * lax.rem(y, 2)
        elif ky == 2:
            yy = lax.rem(y + 2, 4)
        else:
            yy = 3 - y
        cc = core if kc == 0 else 1 - core
        return yy, cc

    def group_dev(k):
        yy, cc = flip(k)
        return (x, expert_at(yy, z, cc))

    def group_pos(k):
        yy, cc = flip(k)
        return yy * NC + cc

    partners = [z_dev(d) for d in range(1, NZ)] + [x_up, x_down] + [group_dev(k) for k in range(1, GROUP)]

    def remote(src, dst, ssem, rsem, dev):
        return pltpu.make_async_remote_copy(
            src_ref=src, dst_ref=dst, send_sem=ssem, recv_sem=rsem,
            device_id=dev, device_id_type=pl.DeviceIdType.MESH,
        )

    loads = [
        pltpu.make_async_copy(a, b, in_sem.at[i])
        for i, (a, b) in enumerate([
            (grads_hbm, grads_ref), (routes_hbm, routes_ref), (weight_hbm, weight_ref), (hot_hbm, hot_ref),
            (inputs_hbm, inputs_raw),
        ])
    ]
    for load in loads:
        load.start()
    barrier = pltpu.get_barrier_semaphore()
    for dev in partners:
        pl.semaphore_signal(barrier, inc=1, device_id=dev, device_id_type=pl.DeviceIdType.MESH)
    pending = []

    def start(copy):
        copy.start()
        pending.append(copy)
        return copy

    H = TOK // 2

    def token_copy(step, up, half):
        lo = half * H
        base = 0 if up else TOK
        if step == 1:
            src = grads_ref.at[pl.ds(lo, H)]
        else:
            src = tokens.at[step - 2, pl.ds(base + lo, H)]
        if step == HALF:
            dst = tokens.at[HALF - 1, pl.ds(TOK + lo, H)]
        else:
            dst = tokens.at[step - 1, pl.ds(base + lo, H)]
        d = 0 if up else 1
        return remote(
            src, dst, tok_send.at[d, step - 1, half], tok_recv.at[d, step - 1, half],
            z_up if up else z_down,
        )

    tok = {}
    for step in range(1, HALF):
        for half in range(2):
            for up in (True, False):
                tok[step, up, half] = token_copy(step, up, half)
    tok[HALF, True, 0] = token_copy(HALF, True, 0)
    tok[HALF, False, 1] = token_copy(HALF, False, 1)

    for load in loads[1:4]:
        load.wait()

    chosen = routes_ref[...]
    erow = iota((EXPERTS, TOK), 0)
    tcol = iota((EXPERTS, TOK), 1)
    onehot = jnp.zeros((EXPERTS, TOK), F32)
    for k in range(TOP):
        onehot += jnp.where(erow == chosen[k:k + 1, :], 1.0, 0.0)
    earlier = jnp.where(erow < tcol, 1.0, 0.0).astype(BF16)
    before = mm(onehot.astype(BF16), earlier)
    hot = jnp.sum(jnp.where(erow == tcol, jnp.broadcast_to(hot_ref[...].astype(F32), (EXPERTS, TOK)), 0.0),
                  axis=1, keepdims=True)
    limit = jnp.where(hot > 0.5, float(SLOTS), float(CAP))
    ranked = jnp.where(before < limit, before, 1000.0)
    zrow = iota((NZ, TOK), 0)
    irow = lax.rem(iota((TOK, TOK), 0), GROUP * SLOTS).astype(F32)
    token = (iota((NZ, TOK), 1) + 1).astype(F32)
    lefts, rights = [], []
    for k in range(TOP):
        e = chosen[k:k + 1, :]
        rank = jnp.sum(jnp.where(erow == e, ranked, 0.0), axis=0, keepdims=True)
        at = (((e // (NZ * NC)) * NC + lax.rem(e, NC)) * SLOTS).astype(F32) + rank
        here = zrow == lax.rem(e // NC, NZ)
        w = weight_ref[k:k + 1, :]
        w1 = w.astype(BF16).astype(F32)
        w2 = (w - w1).astype(BF16).astype(F32)
        w3 = w - w1 - w2
        lefts.append(jnp.concatenate(
            [jnp.where(here, v, 0.0) for v in (token, w1, w2, w3)], axis=0).astype(BF16))
        rights.append(jnp.where(irow == at, 1.0, 0.0).astype(BF16))
    found = lax.dot_general(jnp.concatenate(lefts, axis=1), jnp.concatenate(rights, axis=1),
                            (((1,), (1,)), ((), ())), preferred_element_type=F32)
    weights = found[NZ:2 * NZ] + found[2 * NZ:3 * NZ] + found[3 * NZ:4 * NZ]
    listing = jnp.where(iota((NZ, TOK), 1) < GROUP * SLOTS, found[0:NZ] - 1.0, weights)
    for zz in range(NZ):
        table[zz] = listing[zz:zz + 1, :]

    def table_copy(d):
        return remote(table.at[lax.rem(z + d, NZ)], table_in.at[z], tab_send.at[d], tab_recv.at[d], z_dev(d))

    pl.semaphore_wait(barrier, len(partners))
    for d in (1, 15, 2, 14, 3, 13, 4, 12, 5, 11, 6, 10, 7, 9, 8):
        start(table_copy(d))
    loads[0].wait()
    for half in range(2):
        for up in (True, False):
            start(tok[1, up, half])
    table_in[z] = table[z]

    def advance(step, half):
        for up in (True, False):
            if (step, up, half) in tok:
                tok[step, up, half].wait_recv()
                if (step + 1, up, half) in tok:
                    start(tok[step + 1, up, half])

    ri = iota((GROUP * 2 * SLOTS, TOK), 0)
    rl = iota((GROUP * 2 * SLOTS, TOK), 1)
    from_l = lax.rem(ri // SLOTS, 2) == 0
    rslot = (ri // (2 * SLOTS)) * SLOTS + lax.rem(ri, SLOTS)
    at_token = rl == rslot
    at_weight = rl == rslot + GROUP * SLOTS
    lane = rl.astype(F32)

    def dispatch(pair):
        t_l, t_r = table_in[lax.rem(z + NZ - 1 - pair, NZ)], table_in[lax.rem(z + 1 + pair, NZ)]
        g_l = tokens[pair, 0:TOK]
        g_r = tokens[pair, TOK:2 * TOK]
        both = jnp.where(from_l, t_l, t_r)
        token_of = jnp.sum(jnp.where(at_token, both, 0.0), axis=1, keepdims=True)
        weight = jnp.sum(jnp.where(at_weight, both, 0.0), axis=1, keepdims=True)
        hit = jnp.where(lane == token_of, 1.0, 0.0)
        s_l = jnp.where(from_l, hit, 0.0).astype(BF16)
        s_r = jnp.where(from_l, 0.0, hit).astype(BF16)
        rows = ((mm(s_l, g_l) + mm(s_r, g_r)) * weight).astype(BF16)
        rows_out[pair] = rows.reshape(GROUP, 2 * SLOTS, WIDTH)
        for k in (4, 5, 2, 3, 6, 7, 1):
            start(row_copy(pair, k))
        rows_in[pair, 0] = rows_out[pair, j]

    def single_choice(i):
        t = table_in[lax.rem(z + i * HALF, NZ)]
        token_of = jnp.sum(jnp.where(at_token, t, 0.0), axis=1, keepdims=True)
        weight = jnp.sum(jnp.where(at_weight, t, 0.0), axis=1, keepdims=True)
        return jnp.where(lane == token_of, 1.0, 0.0).astype(BF16), weight

    def dispatch_single(i, hit, weight):
        half = WIDTH // 2
        g = tokens[HALF - 1, TOK:2 * TOK] if i else grads_ref[...]
        found = mm(hit, g)
        first = lax.rem(iota((GROUP * 2 * SLOTS, half), 0) // SLOTS, 2) == 0
        rows = (jnp.where(first, found[:, 0:half], found[:, half:WIDTH]) * weight).astype(BF16)
        fold_out[i] = rows.reshape(GROUP, 2 * SLOTS, half)
        for k in (4, 5, 2, 3, 6, 7, 1):
            start(fold_copy(i, k))
        fold_in[i, 0] = fold_out[i, j]

    def fold_copy(i, k):
        return remote(fold_out.at[i, group_pos(k)], fold_in.at[i, k],
                      fold_send.at[i, k], fold_recv.at[i, k], group_dev(k))

    def unfold_rows():
        whole = []
        for i in range(2):
            for k in range(1, GROUP):
                fold_copy(i, k).wait_recv()
            f = fold_in[i].astype(F32)
            whole.append(jnp.concatenate([f[:, 0:SLOTS], f[:, SLOTS:2 * SLOTS]], axis=2))
        rows_in[HALF - 1] = jnp.concatenate(whole, axis=1).astype(BF16)

    def row_copy(pair, k):
        return remote(rows_out.at[pair, group_pos(k)], rows_in.at[pair, k],
                      row_send.at[pair, k], row_recv.at[pair, k], group_dev(k))

    def send_counts():
        for d in range(1, NZ):
            table_copy(d).wait_recv()
        used = jnp.where(table_in[...].reshape(NZ, TOK) >= 0.0, 1.0, 0.0).astype(BF16)
        src = iota((TOK, TOK), 0)
        hosted = iota((TOK, TOK), 1) >= TOK // 2
        for jj in range(GROUP):
            want = jnp.where(hosted, jj ^ (GROUP // 2), jj)
            counts[jj] = mm(used, jnp.where(src // SLOTS == want, 1.0, 0.0).astype(BF16))
        for k in range(1, GROUP):
            start(cnt_copy(k))
        counts_in[j] = counts[j]

    def cnt_copy(k):
        return remote(counts.at[group_pos(k)], counts_in.at[j], cnt_send.at[k], cnt_recv.at[k], group_dev(k))

    def masks():
        for k in range(1, GROUP):
            cnt_copy(k).wait_recv()
        per = counts_in[...].reshape(EXPERTS, TOK).astype(BF16)
        rr = EXPERTS * SLOTS
        source = iota((rr, EXPERTS), 0) // SLOTS
        m = iota((rr, EXPERTS), 1)
        place = ((m // (NC * NZ)) * NZ + lax.rem(m, NZ)) * NC + lax.rem(m // NZ, NC)
        spread = jnp.where(source == place, 1.0, 0.0).astype(BF16)
        each = mm(spread, per).astype(BF16)
        slot = lax.rem(iota((rr, TOK), 0), SLOTS)
        for i in range(2):
            pickone = jnp.where(iota((TOK, TOK), 0) == i * (TOK // 2), 1.0, 0.0).astype(BF16)
            many = mm(each, pickone)
            good = (many > slot.astype(F32)) & ((slot >= CAP) if i else (slot < CAP))
            keep[i] = jnp.where(good, 1.0, 0.0).astype(BF16)

    def unfold(part):
        step = 8
        count = EXPERTS // step

        def body(i, carry):
            at = pl.multiple_of(i * step * CAP, step * CAP)
            inputs_ref[pl.ds(at, step * CAP), :] = inputs_raw[pl.ds(i * step, step)].reshape(step * CAP, HIDDEN)
            return carry

        lax.fori_loop(part * count, (part + 1) * count, body, 0)

    def input_gram(gram, which, i):
        block = 256
        cols = pl.ds(i * block, block)
        kept = jnp.concatenate([keep[which]] * (block // TOK), axis=1)
        gram[cols, :] = lax.dot_general(
            inputs_ref[:, cols] * kept, inputs_ref[...], TN, preferred_element_type=F32)

    class Scatter:
        def __init__(self, gram, rows, out, via, l_in, r_in, ssem, rsem):
            self.gram, self.rows, self.out, self.via = gram, rows, out, via
            self.l_in, self.r_in, self.ssem, self.rsem = l_in, r_in, ssem, rsem
            self.h = rows // 2

        def part(self, blk, half):
            at = pl.multiple_of(blk * self.rows + half * self.h, 32)
            return self.gram[pl.ds(at, self.h), :]

        def copies(self):
            h = self.h
            lo, hi = pl.ds(0, h), pl.ds(h, h)
            ends = [
                (self.via.at[0], x_up), (self.via.at[1], x_down),
                (self.l_in.at[hi], x_up), (self.r_in.at[lo], x_down),
                (self.l_in.at[lo], x_up), (self.r_in.at[hi], x_down),
            ]
            return [remote(self.out.at[i], dst, self.ssem.at[i], self.rsem.at[i], dev)
                    for i, (dst, dev) in enumerate(ends)]

        def first(self, ready=None):
            self.c = self.copies()
            opposite = lax.rem(x + 2, NX)
            nxt, prv = lax.rem(x + 1, NX), lax.rem(x + NX - 1, NX)
            if ready is not None:
                ready(opposite)
            self.out[0] = self.part(opposite, 0).astype(BF16)
            start(self.c[0])
            self.out[1] = self.part(opposite, 1).astype(BF16)
            start(self.c[1])
            if ready is not None:
                ready(nxt)
            self.out[2] = self.part(nxt, 1).astype(BF16)
            start(self.c[2])
            if ready is not None:
                ready(prv)
            self.out[3] = self.part(prv, 0).astype(BF16)
            start(self.c[3])
            if ready is not None:
                ready(x)

        def second(self):
            nxt, prv = lax.rem(x + 1, NX), lax.rem(x + NX - 1, NX)
            self.c[0].wait_recv()
            self.out[4] = (self.part(nxt, 0) + self.via[0].astype(F32)).astype(BF16)
            start(self.c[4])
            self.c[1].wait_recv()
            self.out[5] = (self.part(prv, 1) + self.via[1].astype(F32)).astype(BF16)
            start(self.c[5])

        def last(self, put):
            h = self.h
            lo, hi = pl.ds(0, h), pl.ds(h, h)
            self.c[2].wait_recv()
            self.c[3].wait_recv()
            self.c[4].wait_recv()
            put(lo, self.part(x, 0) + self.l_in[lo].astype(F32) + self.r_in[lo].astype(F32))
            self.c[5].wait_recv()
            put(hi, self.part(x, 1) + self.l_in[hi].astype(F32) + self.r_in[hi].astype(F32))

    factor = 1.0 / (TOK * TOP * NX)

    own = Scatter(gram_o, HIDDEN // NX, os_out, os_via, os_l, os_r, osem_s, osem_r)
    rep = Scatter(gram_r, HIDDEN // NX, rs_out, rs_via, rs_l, rs_r, rsem_s, rsem_r)
    gs = Scatter(gram_g, WIDTH // NX, gs_out, gs_via, gs_l, gs_r, gsem_s, gsem_r)

    def rows_ready(first_pair, pairs):
        for p in range(first_pair, first_pair + pairs):
            for k in range(1, GROUP):
                row_copy(p, k).wait_recv()

    def gram_rows(first_pair, pairs, blk, fresh):
        kk = pairs * GROUP * 2 * SLOTS
        at = pl.multiple_of(blk * 256, 256)
        a = rows_in[first_pair:first_pair + pairs, :, :, pl.ds(at, 256)].reshape(kk, 256)
        b = rows_in[first_pair:first_pair + pairs].reshape(kk, WIDTH)
        r = lax.dot_general(a, b, TN, preferred_element_type=F32)
        if fresh:
            gram_g[pl.ds(at, 256), :] = r
        else:
            gram_g[pl.ds(at, 256), :] += r

    def gram_part(first_pair, pairs, fresh):
        rows_ready(first_pair, pairs)

        def body(i, carry):
            gram_rows(first_pair, pairs, i, fresh)
            return carry

        lax.fori_loop(0, WIDTH // 256, body, 0)

    far = remote(mine, theirs, far_sem.at[0], far_sem.at[1], group_dev(4))

    saves = []

    def save(src, dst, at, first):
        copy = pltpu.make_async_copy(src.at[at], dst.at[at, 0], out_sem.at[first + (1 if at.start else 0)])
        copy.start()
        saves.append(copy)

    def put_mine(at, value):
        mine[at, :] = value.astype(BF16)

    def put_input(at, value):
        input_out[at, :] = (value + theirs[at, :].astype(F32)) * factor
        save(input_out, input_hbm, at, 0)

    def put_grad(at, value):
        grad_out[at, :] = value * factor
        save(grad_out, grad_hbm, at, 2)

    loads[4].wait()
    advance(1, 0)
    send_counts()
    advance(1, 1)
    dispatch_single(0, *single_choice(0))
    dispatch(0)
    advance(2, 0)
    masks()
    unfold(0)
    advance(2, 1)
    dispatch(1)
    unfold(1)
    advance(3, 0)
    input_gram(gram_r, 1, 0)
    input_gram(gram_r, 1, 1)
    input_gram(gram_r, 1, 2)
    rep.first()
    advance(3, 1)
    dispatch(2)
    input_gram(gram_o, 0, 0)
    advance(4, 0)
    input_gram(gram_o, 0, 1)
    input_gram(gram_o, 0, 2)
    advance(4, 1)
    dispatch(3)
    rep.second()
    advance(5, 0)
    own.first()
    rep.last(put_mine)
    start(far)
    advance(5, 1)
    dispatch(4)
    advance(6, 0)
    gram_part(0, 2, True)
    advance(6, 1)
    dispatch(5)
    own.second()
    advance(7, 0)
    gram_part(2, 2, False)
    advance(7, 1)
    dispatch(6)
    last_choice = single_choice(1)
    advance(8, 0)
    advance(8, 1)
    dispatch_single(1, *last_choice)
    far.wait_recv()
    own.last(put_input)
    gram_part(4, 3, False)
    unfold_rows()
    gs.first(lambda blk: gram_rows(7, 1, blk, False))
    gs.second()
    gs.last(put_grad)
    for copy in pending:
        copy.wait_send()
    for copy in saves:
        copy.wait()


def shards(grads, route_weight, routes, hot, expert_inputs):
    inputs = expert_inputs.reshape(EXPERTS * 2, CAP, HIDDEN)
    hbm = pl.BlockSpec(memory_space=pl.ANY)
    dma = pltpu.SemaphoreType.DMA
    hg, hx = WIDTH // NX // 2, HIDDEN // NX // 2
    grad_factor, input_factor = pl.pallas_call(
        kernel,
        out_shape=(
            jax.ShapeDtypeStruct((WIDTH // NX, 1, WIDTH), F32),
            jax.ShapeDtypeStruct((HIDDEN // NX, 1, HIDDEN), F32),
        ),
        in_specs=[hbm] * 5,
        out_specs=(hbm, hbm),
        scratch_shapes=[
            pltpu.VMEM((TOP, TOK), jnp.int32),
            pltpu.VMEM((TOP, TOK), F32),
            pltpu.VMEM((1, EXPERTS), jnp.int32),
            pltpu.VMEM((TOK, WIDTH), BF16),
            pltpu.VMEM((WIDTH // NX, WIDTH), F32),
            pltpu.VMEM((HIDDEN // NX, HIDDEN), F32),
            dma((4,)),
            pltpu.VMEM((EXPERTS * 2, CAP, HIDDEN), BF16),
            pltpu.VMEM((EXPERTS * SLOTS, HIDDEN), BF16),
            dma((5,)),
            pltpu.VMEM((HALF, 2 * TOK, WIDTH), BF16),
            pltpu.VMEM((NZ, 1, TOK), F32),
            pltpu.VMEM((NZ, 1, TOK), F32),
            pltpu.VMEM((2, EXPERTS * SLOTS, TOK), BF16),
            pltpu.VMEM((GROUP, NZ, TOK), F32),
            pltpu.VMEM((GROUP, NZ, TOK), F32),
            pltpu.VMEM((HALF, GROUP, 2 * SLOTS, WIDTH), BF16),
            pltpu.VMEM((HALF, GROUP, 2 * SLOTS, WIDTH), BF16),
            pltpu.VMEM((2, GROUP, 2 * SLOTS, WIDTH // 2), BF16),
            pltpu.VMEM((2, GROUP, 2 * SLOTS, WIDTH // 2), BF16),
            dma((2, GROUP)), dma((2, GROUP)),
            pltpu.VMEM((WIDTH, WIDTH), F32),
            pltpu.VMEM((HIDDEN, HIDDEN), F32),
            pltpu.VMEM((HIDDEN, HIDDEN), F32),
            pltpu.VMEM((2 * hx, HIDDEN), BF16),
            pltpu.VMEM((2 * hx, HIDDEN), BF16),
            pltpu.VMEM((6, hg, WIDTH), BF16),
            pltpu.VMEM((2, hg, WIDTH), BF16),
            pltpu.VMEM((2 * hg, WIDTH), BF16),
            pltpu.VMEM((2 * hg, WIDTH), BF16),
            pltpu.VMEM((6, hx, HIDDEN), BF16),
            pltpu.VMEM((2, hx, HIDDEN), BF16),
            pltpu.VMEM((2 * hx, HIDDEN), BF16),
            pltpu.VMEM((2 * hx, HIDDEN), BF16),
            pltpu.VMEM((6, hx, HIDDEN), BF16),
            pltpu.VMEM((2, hx, HIDDEN), BF16),
            pltpu.VMEM((2 * hx, HIDDEN), BF16),
            pltpu.VMEM((2 * hx, HIDDEN), BF16),
            dma((2, HALF, 2)), dma((2, HALF, 2)),
            dma((NZ,)), dma((NZ,)),
            dma((2,)),
            dma((GROUP,)), dma((GROUP,)),
            dma((HALF, GROUP)), dma((HALF, GROUP)),
            dma((6,)), dma((6,)), dma((6,)), dma((6,)), dma((6,)), dma((6,)),
        ],
        compiler_params=pltpu.CompilerParams(
            collective_id=0, has_side_effects=True, vmem_limit_bytes=60 * 1024 * 1024
        ),
    )(routes.T, route_weight.T, hot.reshape(1, EXPERTS), grads, inputs)
    return input_factor, grad_factor


def solution(mesh):
    return jax.shard_map(
        shards,
        mesh=mesh,
        in_specs=(
            P(("dp", "expert"), None),
            P(("dp", "expert"), None),
            P(("dp", "expert"), None),
            P(),
            P("dp", "expert", None, None, None, None, None),
        ),
        out_specs=(P("dp", "expert", None), P("dp", "expert", None)),
        check_vma=False,
    )
```

```python
import jax
import jax.numpy as jnp
from jax import lax
from jax.experimental import pallas as pl
from jax.experimental.pallas import tpu as pltpu
from jax.sharding import PartitionSpec as P

NY, NZ, NC, NX = 4, 16, 2, 4
GROUP = NY * NC
HALF = NZ // 2
TOK, TOP, EXPERTS, CAP = 128, 8, 128, 4
WIDTH, HIDDEN = 1024, 768
SLOTS = 2 * CAP
F32, BF16 = jnp.float32, jnp.bfloat16
TN = (((0,), (0,)), ((), ()))


def mm(a, b):
    return jnp.dot(a, b, preferred_element_type=F32)


def iota(shape, dim):
    return lax.broadcasted_iota(jnp.int32, shape, dim)


def kernel(
    routes_hbm, weight_hbm, hot_hbm, grads_hbm, inputs_hbm,
    grad_hbm, input_hbm,
    routes_ref, weight_ref, hot_ref, grads_ref, grad_out, input_out, out_sem, inputs_raw, inputs_ref, in_sem, tokens, table, table_in, keep, counts, counts_in,
    rows_out, rows_in, fold_out, fold_in, fold_send, fold_recv, gram_g, gram_o, gram_r, mine, theirs,
    gs_out, gs_via, gs_l, gs_r, os_out, os_via, os_l, os_r, rs_out, rs_via, rs_l, rs_r,
    tok_send, tok_recv, tab_send, tab_recv, far_sem, cnt_send, cnt_recv,
    row_send, row_recv, gsem_s, gsem_r, osem_s, osem_r, rsem_s, rsem_r,
):
    x = lax.axis_index("dp")
    n = lax.axis_index("expert")
    core = lax.rem(n, NC)
    z = lax.rem(n // NC, NZ)
    y = n // (NC * NZ)
    j = y * NC + core

    def expert_at(yy, zz, cc):
        return (yy * NZ + zz) * NC + cc

    def z_dev(d):
        return (x, expert_at(y, lax.rem(z + d, NZ), core))

    z_up, z_down = z_dev(1), z_dev(NZ - 1)
    x_up = (lax.rem(x + 1, NX), n)
    x_down = (lax.rem(x + NX - 1, NX), n)

    def flip(k):
        ky, kc = k // NC, k % NC
        if ky == 0:
            yy = y
        elif ky == 1:
            yy = y + 1 - 2 * lax.rem(y, 2)
        elif ky == 2:
            yy = lax.rem(y + 2, 4)
        else:
            yy = 3 - y
        cc = core if kc == 0 else 1 - core
        return yy, cc

    def group_dev(k):
        yy, cc = flip(k)
        return (x, expert_at(yy, z, cc))

    def group_pos(k):
        yy, cc = flip(k)
        return yy * NC + cc

    partners = [z_dev(d) for d in range(1, NZ)] + [x_up, x_down] + [group_dev(k) for k in range(1, GROUP)]

    def remote(src, dst, ssem, rsem, dev):
        return pltpu.make_async_remote_copy(
            src_ref=src, dst_ref=dst, send_sem=ssem, recv_sem=rsem,
            device_id=dev, device_id_type=pl.DeviceIdType.MESH,
        )

    loads = [
        pltpu.make_async_copy(a, b, in_sem.at[i])
        for i, (a, b) in enumerate([
            (grads_hbm, grads_ref), (routes_hbm, routes_ref), (weight_hbm, weight_ref), (hot_hbm, hot_ref),
            (inputs_hbm, inputs_raw),
        ])
    ]
    for load in loads:
        load.start()
    barrier = pltpu.get_barrier_semaphore()
    for dev in partners:
        pl.semaphore_signal(barrier, inc=1, device_id=dev, device_id_type=pl.DeviceIdType.MESH)
    pending = []

    def start(copy):
        copy.start()
        pending.append(copy)
        return copy

    H = TOK // 2

    def token_copy(step, up, half):
        lo = half * H
        base = 0 if up else TOK
        if step == 1:
            src = grads_ref.at[pl.ds(lo, H)]
        else:
            src = tokens.at[step - 2, pl.ds(base + lo, H)]
        if step == HALF:
            dst = tokens.at[HALF - 1, pl.ds(TOK + lo, H)]
        else:
            dst = tokens.at[step - 1, pl.ds(base + lo, H)]
        d = 0 if up else 1
        return remote(
            src, dst, tok_send.at[d, step - 1, half], tok_recv.at[d, step - 1, half],
            z_up if up else z_down,
        )

    tok = {}
    for step in range(1, HALF):
        for half in range(2):
            for up in (True, False):
                tok[step, up, half] = token_copy(step, up, half)
    tok[HALF, True, 0] = token_copy(HALF, True, 0)
    tok[HALF, False, 1] = token_copy(HALF, False, 1)

    for load in loads[1:4]:
        load.wait()

    chosen = routes_ref[...]
    erow = iota((EXPERTS, TOK), 0)
    tcol = iota((EXPERTS, TOK), 1)
    onehot = jnp.zeros((EXPERTS, TOK), F32)
    for k in range(TOP):
        onehot += jnp.where(erow == chosen[k:k + 1, :], 1.0, 0.0)
    earlier = jnp.where(erow < tcol, 1.0, 0.0).astype(BF16)
    before = mm(onehot.astype(BF16), earlier)
    hot = jnp.sum(jnp.where(erow == tcol, jnp.broadcast_to(hot_ref[...].astype(F32), (EXPERTS, TOK)), 0.0),
                  axis=1, keepdims=True)
    limit = jnp.where(hot > 0.5, float(SLOTS), float(CAP))
    ranked = jnp.where(before < limit, before, 1000.0)
    zrow = iota((NZ, TOK), 0)
    irow = lax.rem(iota((TOK, TOK), 0), GROUP * SLOTS).astype(F32)
    token = (iota((NZ, TOK), 1) + 1).astype(F32)
    lefts, rights = [], []
    for k in range(TOP):
        e = chosen[k:k + 1, :]
        rank = jnp.sum(jnp.where(erow == e, ranked, 0.0), axis=0, keepdims=True)
        at = (((e // (NZ * NC)) * NC + lax.rem(e, NC)) * SLOTS).astype(F32) + rank
        here = zrow == lax.rem(e // NC, NZ)
        w = weight_ref[k:k + 1, :]
        w1 = w.astype(BF16).astype(F32)
        w2 = (w - w1).astype(BF16).astype(F32)
        w3 = w - w1 - w2
        lefts.append(jnp.concatenate(
            [jnp.where(here, v, 0.0) for v in (token, w1, w2, w3)], axis=0).astype(BF16))
        rights.append(jnp.where(irow == at, 1.0, 0.0).astype(BF16))
    found = lax.dot_general(jnp.concatenate(lefts, axis=1), jnp.concatenate(rights, axis=1),
                            (((1,), (1,)), ((), ())), preferred_element_type=F32)
    weights = found[NZ:2 * NZ] + found[2 * NZ:3 * NZ] + found[3 * NZ:4 * NZ]
    listing = jnp.where(iota((NZ, TOK), 1) < GROUP * SLOTS, found[0:NZ] - 1.0, weights)
    for zz in range(NZ):
        table[zz] = listing[zz:zz + 1, :]

    def table_copy(d):
        return remote(table.at[lax.rem(z + d, NZ)], table_in.at[z], tab_send.at[d], tab_recv.at[d], z_dev(d))

    pl.semaphore_wait(barrier, len(partners))
    for d in (1, 15, 2, 14, 3, 13, 4, 12, 5, 11, 6, 10, 7, 9, 8):
        start(table_copy(d))
    loads[0].wait()
    for half in range(2):
        for up in (True, False):
            start(tok[1, up, half])
    table_in[z] = table[z]

    def advance(step, half):
        for up in (True, False):
            if (step, up, half) in tok:
                tok[step, up, half].wait_recv()
                if (step + 1, up, half) in tok:
                    start(tok[step + 1, up, half])

    ri = iota((GROUP * 2 * SLOTS, TOK), 0)
    rl = iota((GROUP * 2 * SLOTS, TOK), 1)
    from_l = lax.rem(ri // SLOTS, 2) == 0
    rslot = (ri // (2 * SLOTS)) * SLOTS + lax.rem(ri, SLOTS)
    at_token = rl == rslot
    at_weight = rl == rslot + GROUP * SLOTS
    lane = rl.astype(F32)

    def dispatch(pair):
        t_l, t_r = table_in[lax.rem(z + NZ - 1 - pair, NZ)], table_in[lax.rem(z + 1 + pair, NZ)]
        g_l = tokens[pair, 0:TOK]
        g_r = tokens[pair, TOK:2 * TOK]
        both = jnp.where(from_l, t_l, t_r)
        token_of = jnp.sum(jnp.where(at_token, both, 0.0), axis=1, keepdims=True)
        weight = jnp.sum(jnp.where(at_weight, both, 0.0), axis=1, keepdims=True)
        hit = jnp.where(lane == token_of, 1.0, 0.0)
        s_l = jnp.where(from_l, hit, 0.0).astype(BF16)
        s_r = jnp.where(from_l, 0.0, hit).astype(BF16)
        rows = ((mm(s_l, g_l) + mm(s_r, g_r)) * weight).astype(BF16)
        rows_out[pair] = rows.reshape(GROUP, 2 * SLOTS, WIDTH)
        for k in (4, 5, 2, 3, 6, 7, 1):
            start(row_copy(pair, k))
        rows_in[pair, 0] = rows_out[pair, j]

    def single_choice(i):
        t = table_in[lax.rem(z + i * HALF, NZ)]
        token_of = jnp.sum(jnp.where(at_token, t, 0.0), axis=1, keepdims=True)
        weight = jnp.sum(jnp.where(at_weight, t, 0.0), axis=1, keepdims=True)
        return jnp.where(lane == token_of, 1.0, 0.0).astype(BF16), weight

    def dispatch_single(i, hit, weight):
        half = WIDTH // 2
        g = tokens[HALF - 1, TOK:2 * TOK] if i else grads_ref[...]
        found = mm(hit, g)
        first = lax.rem(iota((GROUP * 2 * SLOTS, half), 0) // SLOTS, 2) == 0
        rows = (jnp.where(first, found[:, 0:half], found[:, half:WIDTH]) * weight).astype(BF16)
        fold_out[i] = rows.reshape(GROUP, 2 * SLOTS, half)
        for k in (4, 5, 2, 3, 6, 7, 1):
            start(fold_copy(i, k))
        fold_in[i, 0] = fold_out[i, j]

    def fold_copy(i, k):
        return remote(fold_out.at[i, group_pos(k)], fold_in.at[i, k],
                      fold_send.at[i, k], fold_recv.at[i, k], group_dev(k))

    def unfold_rows():
        whole = []
        for i in range(2):
            for k in range(1, GROUP):
                fold_copy(i, k).wait_recv()
            f = fold_in[i].astype(F32)
            whole.append(jnp.concatenate([f[:, 0:SLOTS], f[:, SLOTS:2 * SLOTS]], axis=2))
        rows_in[HALF - 1] = jnp.concatenate(whole, axis=1).astype(BF16)

    def row_copy(pair, k):
        return remote(rows_out.at[pair, group_pos(k)], rows_in.at[pair, k],
                      row_send.at[pair, k], row_recv.at[pair, k], group_dev(k))

    def send_counts():
        for d in range(1, NZ):
            table_copy(d).wait_recv()
        used = jnp.where(table_in[...].reshape(NZ, TOK) >= 0.0, 1.0, 0.0).astype(BF16)
        src = iota((TOK, TOK), 0)
        hosted = iota((TOK, TOK), 1) >= TOK // 2
        for jj in range(GROUP):
            want = jnp.where(hosted, jj ^ (GROUP // 2), jj)
            counts[jj] = mm(used, jnp.where(src // SLOTS == want, 1.0, 0.0).astype(BF16))
        for k in range(1, GROUP):
            start(cnt_copy(k))
        counts_in[j] = counts[j]

    def cnt_copy(k):
        return remote(counts.at[group_pos(k)], counts_in.at[j], cnt_send.at[k], cnt_recv.at[k], group_dev(k))

    def masks():
        for k in range(1, GROUP):
            cnt_copy(k).wait_recv()
        per = counts_in[...].reshape(EXPERTS, TOK).astype(BF16)
        rr = EXPERTS * SLOTS
        source = iota((rr, EXPERTS), 0) // SLOTS
        m = iota((rr, EXPERTS), 1)
        place = ((m // (NC * NZ)) * NZ + lax.rem(m, NZ)) * NC + lax.rem(m // NZ, NC)
        spread = jnp.where(source == place, 1.0, 0.0).astype(BF16)
        each = mm(spread, per).astype(BF16)
        slot = lax.rem(iota((rr, TOK), 0), SLOTS)
        for i in range(2):
            pickone = jnp.where(iota((TOK, TOK), 0) == i * (TOK // 2), 1.0, 0.0).astype(BF16)
            many = mm(each, pickone)
            good = (many > slot.astype(F32)) & ((slot >= CAP) if i else (slot < CAP))
            keep[i] = jnp.where(good, 1.0, 0.0).astype(BF16)

    def unfold(part):
        step = 8
        count = EXPERTS // step

        def body(i, carry):
            at = pl.multiple_of(i * step * CAP, step * CAP)
            inputs_ref[pl.ds(at, step * CAP), :] = inputs_raw[pl.ds(i * step, step)].reshape(step * CAP, HIDDEN)
            return carry

        lax.fori_loop(part * count, (part + 1) * count, body, 0)

    def input_gram(gram, which, i):
        block = 256
        cols = pl.ds(i * block, block)
        kept = jnp.concatenate([keep[which]] * (block // TOK), axis=1)
        gram[cols, :] = lax.dot_general(
            inputs_ref[:, cols] * kept, inputs_ref[...], TN, preferred_element_type=F32)

    class Scatter:
        def __init__(self, gram, rows, out, via, l_in, r_in, ssem, rsem):
            self.gram, self.rows, self.out, self.via = gram, rows, out, via
            self.l_in, self.r_in, self.ssem, self.rsem = l_in, r_in, ssem, rsem
            self.h = rows // 2

        def part(self, blk, half):
            at = pl.multiple_of(blk * self.rows + half * self.h, 32)
            return self.gram[pl.ds(at, self.h), :]

        def copies(self):
            h = self.h
            lo, hi = pl.ds(0, h), pl.ds(h, h)
            ends = [
                (self.via.at[0], x_up), (self.via.at[1], x_down),
                (self.l_in.at[hi], x_up), (self.r_in.at[lo], x_down),
                (self.l_in.at[lo], x_up), (self.r_in.at[hi], x_down),
            ]
            return [remote(self.out.at[i], dst, self.ssem.at[i], self.rsem.at[i], dev)
                    for i, (dst, dev) in enumerate(ends)]

        def first(self, ready=None):
            self.c = self.copies()
            opposite = lax.rem(x + 2, NX)
            nxt, prv = lax.rem(x + 1, NX), lax.rem(x + NX - 1, NX)
            if ready is not None:
                ready(opposite)
            self.out[0] = self.part(opposite, 0).astype(BF16)
            start(self.c[0])
            self.out[1] = self.part(opposite, 1).astype(BF16)
            start(self.c[1])
            if ready is not None:
                ready(nxt)
            self.out[2] = self.part(nxt, 1).astype(BF16)
            start(self.c[2])
            if ready is not None:
                ready(prv)
            self.out[3] = self.part(prv, 0).astype(BF16)
            start(self.c[3])
            if ready is not None:
                ready(x)

        def second(self):
            nxt, prv = lax.rem(x + 1, NX), lax.rem(x + NX - 1, NX)
            self.c[0].wait_recv()
            self.out[4] = (self.part(nxt, 0) + self.via[0].astype(F32)).astype(BF16)
            start(self.c[4])
            self.c[1].wait_recv()
            self.out[5] = (self.part(prv, 1) + self.via[1].astype(F32)).astype(BF16)
            start(self.c[5])

        def last(self, put):
            h = self.h
            lo, hi = pl.ds(0, h), pl.ds(h, h)
            self.c[2].wait_recv()
            self.c[3].wait_recv()
            self.c[4].wait_recv()
            put(lo, self.part(x, 0) + self.l_in[lo].astype(F32) + self.r_in[lo].astype(F32))
            self.c[5].wait_recv()
            put(hi, self.part(x, 1) + self.l_in[hi].astype(F32) + self.r_in[hi].astype(F32))

    factor = 1.0 / (TOK * TOP * NX)

    own = Scatter(gram_o, HIDDEN // NX, os_out, os_via, os_l, os_r, osem_s, osem_r)
    rep = Scatter(gram_r, HIDDEN // NX, rs_out, rs_via, rs_l, rs_r, rsem_s, rsem_r)
    gs = Scatter(gram_g, WIDTH // NX, gs_out, gs_via, gs_l, gs_r, gsem_s, gsem_r)

    def rows_ready(first_pair, pairs):
        for p in range(first_pair, first_pair + pairs):
            for k in range(1, GROUP):
                row_copy(p, k).wait_recv()

    def gram_rows(first_pair, pairs, blk, fresh):
        kk = pairs * GROUP * 2 * SLOTS
        at = pl.multiple_of(blk * 256, 256)
        a = rows_in[first_pair:first_pair + pairs, :, :, pl.ds(at, 256)].reshape(kk, 256)
        b = rows_in[first_pair:first_pair + pairs].reshape(kk, WIDTH)
        r = lax.dot_general(a, b, TN, preferred_element_type=F32)
        if fresh:
            gram_g[pl.ds(at, 256), :] = r
        else:
            gram_g[pl.ds(at, 256), :] += r

    def gram_part(first_pair, pairs, fresh):
        rows_ready(first_pair, pairs)

        def body(i, carry):
            gram_rows(first_pair, pairs, i, fresh)
            return carry

        lax.fori_loop(0, WIDTH // 256, body, 0)

    far = remote(mine, theirs, far_sem.at[0], far_sem.at[1], group_dev(4))

    saves = []

    def save(src, dst, at, first):
        copy = pltpu.make_async_copy(src.at[at], dst.at[at, 0], out_sem.at[first + (1 if at.start else 0)])
        copy.start()
        saves.append(copy)

    def put_mine(at, value):
        mine[at, :] = value.astype(BF16)

    def put_input(at, value):
        input_out[at, :] = (value + theirs[at, :].astype(F32)) * factor
        save(input_out, input_hbm, at, 0)

    def put_grad(at, value):
        grad_out[at, :] = value * factor
        save(grad_out, grad_hbm, at, 2)

    loads[4].wait()
    advance(1, 0)
    send_counts()
    advance(1, 1)
    dispatch_single(0, *single_choice(0))
    dispatch(0)
    advance(2, 0)
    masks()
    unfold(0)
    advance(2, 1)
    dispatch(1)
    unfold(1)
    advance(3, 0)
    input_gram(gram_r, 1, 0)
    input_gram(gram_r, 1, 1)
    input_gram(gram_r, 1, 2)
    rep.first()
    advance(3, 1)
    dispatch(2)
    input_gram(gram_o, 0, 0)
    advance(4, 0)
    input_gram(gram_o, 0, 1)
    input_gram(gram_o, 0, 2)
    advance(4, 1)
    dispatch(3)
    rep.second()
    advance(5, 0)
    own.first()
    rep.last(put_mine)
    start(far)
    advance(5, 1)
    dispatch(4)
    advance(6, 0)
    gram_part(0, 2, True)
    advance(6, 1)
    dispatch(5)
    own.second()
    advance(7, 0)
    gram_part(2, 2, False)
    advance(7, 1)
    dispatch(6)
    last_choice = single_choice(1)
    advance(8, 0)
    advance(8, 1)
    dispatch_single(1, *last_choice)
    far.wait_recv()
    own.last(put_input)
    gram_part(4, 3, False)
    unfold_rows()
    before_sum = len(pending)
    gs.first(lambda blk: gram_rows(7, 1, blk, False))
    for copy in pending[:before_sum]:
        copy.wait_send()
    gs.second()
    gs.last(put_grad)
    for copy in pending[before_sum:]:
        copy.wait_send()
    for copy in saves:
        copy.wait()


def shards(grads, route_weight, routes, hot, expert_inputs):
    inputs = expert_inputs.reshape(EXPERTS * 2, CAP, HIDDEN)
    hbm = pl.BlockSpec(memory_space=pl.ANY)
    dma = pltpu.SemaphoreType.DMA
    hg, hx = WIDTH // NX // 2, HIDDEN // NX // 2
    grad_factor, input_factor = pl.pallas_call(
        kernel,
        out_shape=(
            jax.ShapeDtypeStruct((WIDTH // NX, 1, WIDTH), F32),
            jax.ShapeDtypeStruct((HIDDEN // NX, 1, HIDDEN), F32),
        ),
        in_specs=[hbm] * 5,
        out_specs=(hbm, hbm),
        scratch_shapes=[
            pltpu.VMEM((TOP, TOK), jnp.int32),
            pltpu.VMEM((TOP, TOK), F32),
            pltpu.VMEM((1, EXPERTS), jnp.int32),
            pltpu.VMEM((TOK, WIDTH), BF16),
            pltpu.VMEM((WIDTH // NX, WIDTH), F32),
            pltpu.VMEM((HIDDEN // NX, HIDDEN), F32),
            dma((4,)),
            pltpu.VMEM((EXPERTS * 2, CAP, HIDDEN), BF16),
            pltpu.VMEM((EXPERTS * SLOTS, HIDDEN), BF16),
            dma((5,)),
            pltpu.VMEM((HALF, 2 * TOK, WIDTH), BF16),
            pltpu.VMEM((NZ, 1, TOK), F32),
            pltpu.VMEM((NZ, 1, TOK), F32),
            pltpu.VMEM((2, EXPERTS * SLOTS, TOK), BF16),
            pltpu.VMEM((GROUP, NZ, TOK), F32),
            pltpu.VMEM((GROUP, NZ, TOK), F32),
            pltpu.VMEM((HALF, GROUP, 2 * SLOTS, WIDTH), BF16),
            pltpu.VMEM((HALF, GROUP, 2 * SLOTS, WIDTH), BF16),
            pltpu.VMEM((2, GROUP, 2 * SLOTS, WIDTH // 2), BF16),
            pltpu.VMEM((2, GROUP, 2 * SLOTS, WIDTH // 2), BF16),
            dma((2, GROUP)), dma((2, GROUP)),
            pltpu.VMEM((WIDTH, WIDTH), F32),
            pltpu.VMEM((HIDDEN, HIDDEN), F32),
            pltpu.VMEM((HIDDEN, HIDDEN), F32),
            pltpu.VMEM((2 * hx, HIDDEN), BF16),
            pltpu.VMEM((2 * hx, HIDDEN), BF16),
            pltpu.VMEM((6, hg, WIDTH), BF16),
            pltpu.VMEM((2, hg, WIDTH), BF16),
            pltpu.VMEM((2 * hg, WIDTH), BF16),
            pltpu.VMEM((2 * hg, WIDTH), BF16),
            pltpu.VMEM((6, hx, HIDDEN), BF16),
            pltpu.VMEM((2, hx, HIDDEN), BF16),
            pltpu.VMEM((2 * hx, HIDDEN), BF16),
            pltpu.VMEM((2 * hx, HIDDEN), BF16),
            pltpu.VMEM((6, hx, HIDDEN), BF16),
            pltpu.VMEM((2, hx, HIDDEN), BF16),
            pltpu.VMEM((2 * hx, HIDDEN), BF16),
            pltpu.VMEM((2 * hx, HIDDEN), BF16),
            dma((2, HALF, 2)), dma((2, HALF, 2)),
            dma((NZ,)), dma((NZ,)),
            dma((2,)),
            dma((GROUP,)), dma((GROUP,)),
            dma((HALF, GROUP)), dma((HALF, GROUP)),
            dma((6,)), dma((6,)), dma((6,)), dma((6,)), dma((6,)), dma((6,)),
        ],
        compiler_params=pltpu.CompilerParams(
            collective_id=0, has_side_effects=True, vmem_limit_bytes=60 * 1024 * 1024
        ),
    )(routes.T, route_weight.T, hot.reshape(1, EXPERTS), grads, inputs)
    return input_factor, grad_factor


def solution(mesh):
    return jax.shard_map(
        shards,
        mesh=mesh,
        in_specs=(
            P(("dp", "expert"), None),
            P(("dp", "expert"), None),
            P(("dp", "expert"), None),
            P(),
            P("dp", "expert", None, None, None, None, None),
        ),
        out_specs=(P("dp", "expert", None), P("dp", "expert", None)),
        check_vma=False,
    )
```

```python
import jax
import jax.numpy as jnp
from jax import lax
from jax.experimental import pallas as pl
from jax.experimental.pallas import tpu as pltpu
from jax.sharding import PartitionSpec as P

NY, NZ, NC, NX = 4, 16, 2, 4
GROUP = NY * NC
HALF = NZ // 2
TOK, TOP, EXPERTS, CAP = 128, 8, 128, 4
WIDTH, HIDDEN = 1024, 768
SLOTS = 2 * CAP
F32, BF16 = jnp.float32, jnp.bfloat16
TN = (((0,), (0,)), ((), ()))


def mm(a, b):
    return jnp.dot(a, b, preferred_element_type=F32)


def iota(shape, dim):
    return lax.broadcasted_iota(jnp.int32, shape, dim)


def kernel(
    routes_hbm, weight_hbm, hot_hbm, grads_hbm, inputs_hbm,
    grad_hbm, input_hbm,
    routes_ref, weight_ref, hot_ref, grads_ref, grad_out, input_out, out_sem, inputs_raw, inputs_ref, in_sem, tokens, table, table_in, keep, counts, counts_in,
    rows_out, rows_in, fold_out, fold_in, fold_send, fold_recv, gram_g, gram_o, gram_r, mine, theirs,
    gs_out, gs_via, gs_l, gs_r, os_out, os_via, os_l, os_r, rs_out, rs_via, rs_l, rs_r,
    tok_send, tok_recv, tab_send, tab_recv, far_sem, cnt_send, cnt_recv,
    row_send, row_recv, gsem_s, gsem_r, osem_s, osem_r, rsem_s, rsem_r,
):
    x = lax.axis_index("dp")
    n = lax.axis_index("expert")
    core = lax.rem(n, NC)
    z = lax.rem(n // NC, NZ)
    y = n // (NC * NZ)
    j = y * NC + core

    def expert_at(yy, zz, cc):
        return (yy * NZ + zz) * NC + cc

    def z_dev(d):
        return (x, expert_at(y, lax.rem(z + d, NZ), core))

    z_up, z_down = z_dev(1), z_dev(NZ - 1)
    x_up = (lax.rem(x + 1, NX), n)
    x_down = (lax.rem(x + NX - 1, NX), n)

    def flip(k):
        ky, kc = k // NC, k % NC
        if ky == 0:
            yy = y
        elif ky == 1:
            yy = y + 1 - 2 * lax.rem(y, 2)
        elif ky == 2:
            yy = lax.rem(y + 2, 4)
        else:
            yy = 3 - y
        cc = core if kc == 0 else 1 - core
        return yy, cc

    def group_dev(k):
        yy, cc = flip(k)
        return (x, expert_at(yy, z, cc))

    def group_pos(k):
        yy, cc = flip(k)
        return yy * NC + cc

    partners = [z_dev(d) for d in range(1, NZ)] + [x_up, x_down] + [group_dev(k) for k in range(1, GROUP)]

    def remote(src, dst, ssem, rsem, dev):
        return pltpu.make_async_remote_copy(
            src_ref=src, dst_ref=dst, send_sem=ssem, recv_sem=rsem,
            device_id=dev, device_id_type=pl.DeviceIdType.MESH,
        )

    loads = [
        pltpu.make_async_copy(a, b, in_sem.at[i])
        for i, (a, b) in enumerate([
            (grads_hbm, grads_ref), (routes_hbm, routes_ref), (weight_hbm, weight_ref), (hot_hbm, hot_ref),
            (inputs_hbm, inputs_raw),
        ])
    ]
    for load in loads:
        load.start()
    barrier = pltpu.get_barrier_semaphore()
    for dev in partners:
        pl.semaphore_signal(barrier, inc=1, device_id=dev, device_id_type=pl.DeviceIdType.MESH)
    pending = []

    def start(copy):
        copy.start()
        pending.append(copy)
        return copy

    H = TOK // 2

    def token_copy(step, up, half):
        lo = half * H
        base = 0 if up else TOK
        if step == 1:
            src = grads_ref.at[pl.ds(lo, H)]
        else:
            src = tokens.at[step - 2, pl.ds(base + lo, H)]
        if step == HALF:
            dst = tokens.at[HALF - 1, pl.ds(TOK + lo, H)]
        else:
            dst = tokens.at[step - 1, pl.ds(base + lo, H)]
        d = 0 if up else 1
        return remote(
            src, dst, tok_send.at[d, step - 1, half], tok_recv.at[d, step - 1, half],
            z_up if up else z_down,
        )

    tok = {}
    for step in range(1, HALF):
        for half in range(2):
            for up in (True, False):
                tok[step, up, half] = token_copy(step, up, half)
    tok[HALF, True, 0] = token_copy(HALF, True, 0)
    tok[HALF, False, 1] = token_copy(HALF, False, 1)

    for load in loads[1:4]:
        load.wait()

    chosen = routes_ref[...]
    erow = iota((EXPERTS, TOK), 0)
    tcol = iota((EXPERTS, TOK), 1)
    onehot = jnp.zeros((EXPERTS, TOK), F32)
    for k in range(TOP):
        onehot += jnp.where(erow == chosen[k:k + 1, :], 1.0, 0.0)
    earlier = jnp.where(erow < tcol, 1.0, 0.0).astype(BF16)
    before = mm(onehot.astype(BF16), earlier)
    hot = jnp.sum(jnp.where(erow == tcol, jnp.broadcast_to(hot_ref[...].astype(F32), (EXPERTS, TOK)), 0.0),
                  axis=1, keepdims=True)
    limit = jnp.where(hot > 0.5, float(SLOTS), float(CAP))
    ranked = jnp.where(before < limit, before, 1000.0)
    zrow = iota((NZ, TOK), 0)
    irow = lax.rem(iota((TOK, TOK), 0), GROUP * SLOTS).astype(F32)
    token = (iota((NZ, TOK), 1) + 1).astype(F32)
    lefts, rights = [], []
    for k in range(TOP):
        e = chosen[k:k + 1, :]
        rank = jnp.sum(jnp.where(erow == e, ranked, 0.0), axis=0, keepdims=True)
        at = (((e // (NZ * NC)) * NC + lax.rem(e, NC)) * SLOTS).astype(F32) + rank
        here = zrow == lax.rem(e // NC, NZ)
        w = weight_ref[k:k + 1, :]
        w1 = w.astype(BF16).astype(F32)
        w2 = (w - w1).astype(BF16).astype(F32)
        w3 = w - w1 - w2
        lefts.append(jnp.concatenate(
            [jnp.where(here, v, 0.0) for v in (token, w1, w2, w3)], axis=0).astype(BF16))
        rights.append(jnp.where(irow == at, 1.0, 0.0).astype(BF16))
    found = lax.dot_general(jnp.concatenate(lefts, axis=1), jnp.concatenate(rights, axis=1),
                            (((1,), (1,)), ((), ())), preferred_element_type=F32)
    weights = found[NZ:2 * NZ] + found[2 * NZ:3 * NZ] + found[3 * NZ:4 * NZ]
    listing = jnp.where(iota((NZ, TOK), 1) < GROUP * SLOTS, found[0:NZ] - 1.0, weights)
    for zz in range(NZ):
        table[zz] = listing[zz:zz + 1, :]

    def table_copy(d):
        return remote(table.at[lax.rem(z + d, NZ)], table_in.at[z], tab_send.at[d], tab_recv.at[d], z_dev(d))

    pl.semaphore_wait(barrier, len(partners))
    for d in (1, 15, 2, 14, 3, 13, 4, 12, 5, 11, 6, 10, 7, 9, 8):
        start(table_copy(d))
    loads[0].wait()
    for half in range(2):
        for up in (True, False):
            start(tok[1, up, half])
    table_in[z] = table[z]

    def advance(step, half):
        for up in (True, False):
            if (step, up, half) in tok:
                tok[step, up, half].wait_recv()
                if (step + 1, up, half) in tok:
                    start(tok[step + 1, up, half])

    ri = iota((GROUP * 2 * SLOTS, TOK), 0)
    rl = iota((GROUP * 2 * SLOTS, TOK), 1)
    from_l = lax.rem(ri // SLOTS, 2) == 0
    rslot = (ri // (2 * SLOTS)) * SLOTS + lax.rem(ri, SLOTS)
    at_token = rl == rslot
    at_weight = rl == rslot + GROUP * SLOTS
    lane = rl.astype(F32)

    def dispatch(pair):
        t_l, t_r = table_in[lax.rem(z + NZ - 1 - pair, NZ)], table_in[lax.rem(z + 1 + pair, NZ)]
        g_l = tokens[pair, 0:TOK]
        g_r = tokens[pair, TOK:2 * TOK]
        both = jnp.where(from_l, t_l, t_r)
        token_of = jnp.sum(jnp.where(at_token, both, 0.0), axis=1, keepdims=True)
        weight = jnp.sum(jnp.where(at_weight, both, 0.0), axis=1, keepdims=True)
        hit = jnp.where(lane == token_of, 1.0, 0.0)
        s_l = jnp.where(from_l, hit, 0.0).astype(BF16)
        s_r = jnp.where(from_l, 0.0, hit).astype(BF16)
        rows = ((mm(s_l, g_l) + mm(s_r, g_r)) * weight).astype(BF16)
        rows_out[pair] = rows.reshape(GROUP, 2 * SLOTS, WIDTH)
        for k in (4, 5, 2, 3, 6, 7, 1):
            start(row_copy(pair, k))
        rows_in[pair, 0] = rows_out[pair, j]

    def single_choice(i):
        t = table_in[lax.rem(z + i * HALF, NZ)]
        token_of = jnp.sum(jnp.where(at_token, t, 0.0), axis=1, keepdims=True)
        weight = jnp.sum(jnp.where(at_weight, t, 0.0), axis=1, keepdims=True)
        return jnp.where(lane == token_of, 1.0, 0.0).astype(BF16), weight

    def dispatch_single(i, hit, weight):
        half = WIDTH // 2
        g = tokens[HALF - 1, TOK:2 * TOK] if i else grads_ref[...]
        found = mm(hit, g)
        first = lax.rem(iota((GROUP * 2 * SLOTS, half), 0) // SLOTS, 2) == 0
        rows = (jnp.where(first, found[:, 0:half], found[:, half:WIDTH]) * weight).astype(BF16)
        fold_out[i] = rows.reshape(GROUP, 2 * SLOTS, half)
        for k in (4, 5, 2, 3, 6, 7, 1):
            start(fold_copy(i, k))
        fold_in[i, 0] = fold_out[i, j]

    def fold_copy(i, k):
        return remote(fold_out.at[i, group_pos(k)], fold_in.at[i, k],
                      fold_send.at[i, k], fold_recv.at[i, k], group_dev(k))

    def unfold_rows():
        whole = []
        for i in range(2):
            for k in range(1, GROUP):
                fold_copy(i, k).wait_recv()
            f = fold_in[i].astype(F32)
            whole.append(jnp.concatenate([f[:, 0:SLOTS], f[:, SLOTS:2 * SLOTS]], axis=2))
        rows_in[HALF - 1] = jnp.concatenate(whole, axis=1).astype(BF16)

    def row_copy(pair, k):
        return remote(rows_out.at[pair, group_pos(k)], rows_in.at[pair, k],
                      row_send.at[pair, k], row_recv.at[pair, k], group_dev(k))

    def send_counts():
        for d in range(1, NZ):
            table_copy(d).wait_recv()
        used = jnp.where(table_in[...].reshape(NZ, TOK) >= 0.0, 1.0, 0.0).astype(BF16)
        src = iota((TOK, TOK), 0)
        hosted = iota((TOK, TOK), 1) >= TOK // 2
        for jj in range(GROUP):
            want = jnp.where(hosted, jj ^ (GROUP // 2), jj)
            counts[jj] = mm(used, jnp.where(src // SLOTS == want, 1.0, 0.0).astype(BF16))
        for k in range(1, GROUP):
            start(cnt_copy(k))
        counts_in[j] = counts[j]

    def cnt_copy(k):
        return remote(counts.at[group_pos(k)], counts_in.at[j], cnt_send.at[k], cnt_recv.at[k], group_dev(k))

    def masks():
        for k in range(1, GROUP):
            cnt_copy(k).wait_recv()
        per = counts_in[...].reshape(EXPERTS, TOK).astype(BF16)
        rr = EXPERTS * SLOTS
        source = iota((rr, EXPERTS), 0) // SLOTS
        m = iota((rr, EXPERTS), 1)
        place = ((m // (NC * NZ)) * NZ + lax.rem(m, NZ)) * NC + lax.rem(m // NZ, NC)
        spread = jnp.where(source == place, 1.0, 0.0).astype(BF16)
        each = mm(spread, per).astype(BF16)
        slot = lax.rem(iota((rr, TOK), 0), SLOTS)
        for i in range(2):
            pickone = jnp.where(iota((TOK, TOK), 0) == i * (TOK // 2), 1.0, 0.0).astype(BF16)
            many = mm(each, pickone)
            good = (many > slot.astype(F32)) & ((slot >= CAP) if i else (slot < CAP))
            keep[i] = jnp.where(good, 1.0, 0.0).astype(BF16)

    def unfold(part):
        step = 8
        count = EXPERTS // step

        def body(i, carry):
            at = pl.multiple_of(i * step * CAP, step * CAP)
            inputs_ref[pl.ds(at, step * CAP), :] = inputs_raw[pl.ds(i * step, step)].reshape(step * CAP, HIDDEN)
            return carry

        lax.fori_loop(part * count, (part + 1) * count, body, 0)

    def input_gram(gram, which, i):
        block = 256
        cols = pl.ds(i * block, block)
        kept = jnp.concatenate([keep[which]] * (block // TOK), axis=1)
        gram[cols, :] = lax.dot_general(
            inputs_ref[:, cols] * kept, inputs_ref[...], TN, preferred_element_type=F32)

    class Scatter:
        def __init__(self, gram, rows, out, via, l_in, r_in, ssem, rsem):
            self.gram, self.rows, self.out, self.via = gram, rows, out, via
            self.l_in, self.r_in, self.ssem, self.rsem = l_in, r_in, ssem, rsem
            self.h = rows // 2

        def part(self, blk, half):
            at = pl.multiple_of(blk * self.rows + half * self.h, 32)
            return self.gram[pl.ds(at, self.h), :]

        def copies(self):
            h = self.h
            lo, hi = pl.ds(0, h), pl.ds(h, h)
            ends = [
                (self.via.at[0], x_up), (self.via.at[1], x_down),
                (self.l_in.at[hi], x_up), (self.r_in.at[lo], x_down),
                (self.l_in.at[lo], x_up), (self.r_in.at[hi], x_down),
            ]
            return [remote(self.out.at[i], dst, self.ssem.at[i], self.rsem.at[i], dev)
                    for i, (dst, dev) in enumerate(ends)]

        def first(self, ready=None):
            self.c = self.copies()
            opposite = lax.rem(x + 2, NX)
            nxt, prv = lax.rem(x + 1, NX), lax.rem(x + NX - 1, NX)
            if ready is not None:
                ready(opposite)
            self.out[0] = self.part(opposite, 0).astype(BF16)
            start(self.c[0])
            self.out[1] = self.part(opposite, 1).astype(BF16)
            start(self.c[1])
            if ready is not None:
                ready(nxt)
            self.out[2] = self.part(nxt, 1).astype(BF16)
            start(self.c[2])
            if ready is not None:
                ready(prv)
            self.out[3] = self.part(prv, 0).astype(BF16)
            start(self.c[3])
            if ready is not None:
                ready(x)

        def second(self):
            nxt, prv = lax.rem(x + 1, NX), lax.rem(x + NX - 1, NX)
            self.c[0].wait_recv()
            self.out[4] = (self.part(nxt, 0) + self.via[0].astype(F32)).astype(BF16)
            start(self.c[4])
            self.c[1].wait_recv()
            self.out[5] = (self.part(prv, 1) + self.via[1].astype(F32)).astype(BF16)
            start(self.c[5])

        def last(self, put):
            h = self.h
            lo, hi = pl.ds(0, h), pl.ds(h, h)
            self.c[2].wait_recv()
            self.c[3].wait_recv()
            low = pl.ds(pl.multiple_of(x * self.rows, 32), h)
            high = pl.ds(pl.multiple_of(x * self.rows + h, 32), h)
            self.gram[low, :] += self.r_in[lo].astype(F32)
            self.gram[high, :] += self.l_in[hi].astype(F32)
            self.c[4].wait_recv()
            put(lo, self.part(x, 0) + self.l_in[lo].astype(F32))
            self.c[5].wait_recv()
            put(hi, self.part(x, 1) + self.r_in[hi].astype(F32))

    factor = 1.0 / (TOK * TOP * NX)

    own = Scatter(gram_o, HIDDEN // NX, os_out, os_via, os_l, os_r, osem_s, osem_r)
    rep = Scatter(gram_r, HIDDEN // NX, rs_out, rs_via, rs_l, rs_r, rsem_s, rsem_r)
    gs = Scatter(gram_g, WIDTH // NX, gs_out, gs_via, gs_l, gs_r, gsem_s, gsem_r)

    def rows_ready(first_pair, pairs):
        for p in range(first_pair, first_pair + pairs):
            for k in range(1, GROUP):
                row_copy(p, k).wait_recv()

    def gram_rows(first_pair, pairs, blk, fresh):
        kk = pairs * GROUP * 2 * SLOTS
        at = pl.multiple_of(blk * 256, 256)
        a = rows_in[first_pair:first_pair + pairs, :, :, pl.ds(at, 256)].reshape(kk, 256)
        b = rows_in[first_pair:first_pair + pairs].reshape(kk, WIDTH)
        r = lax.dot_general(a, b, TN, preferred_element_type=F32)
        if fresh:
            gram_g[pl.ds(at, 256), :] = r
        else:
            gram_g[pl.ds(at, 256), :] += r

    def gram_part(first_pair, pairs, fresh):
        rows_ready(first_pair, pairs)

        def body(i, carry):
            gram_rows(first_pair, pairs, i, fresh)
            return carry

        lax.fori_loop(0, WIDTH // 256, body, 0)

    far = remote(mine, theirs, far_sem.at[0], far_sem.at[1], group_dev(4))

    saves = []

    def save(src, dst, at, first):
        copy = pltpu.make_async_copy(src.at[at], dst.at[at, 0], out_sem.at[first + (1 if at.start else 0)])
        copy.start()
        saves.append(copy)

    def put_mine(at, value):
        mine[at, :] = value.astype(BF16)

    def put_input(at, value):
        input_out[at, :] = (value + theirs[at, :].astype(F32)) * factor
        save(input_out, input_hbm, at, 0)

    def put_grad(at, value):
        grad_out[at, :] = value * factor
        save(grad_out, grad_hbm, at, 2)

    loads[4].wait()
    advance(1, 0)
    send_counts()
    advance(1, 1)
    dispatch_single(0, *single_choice(0))
    dispatch(0)
    advance(2, 0)
    masks()
    unfold(0)
    advance(2, 1)
    dispatch(1)
    unfold(1)
    advance(3, 0)
    input_gram(gram_r, 1, 0)
    input_gram(gram_r, 1, 1)
    input_gram(gram_r, 1, 2)
    rep.first()
    advance(3, 1)
    dispatch(2)
    input_gram(gram_o, 0, 0)
    advance(4, 0)
    input_gram(gram_o, 0, 1)
    input_gram(gram_o, 0, 2)
    advance(4, 1)
    dispatch(3)
    rep.second()
    advance(5, 0)
    own.first()
    rep.last(put_mine)
    start(far)
    advance(5, 1)
    dispatch(4)
    advance(6, 0)
    gram_part(0, 2, True)
    advance(6, 1)
    dispatch(5)
    own.second()
    advance(7, 0)
    gram_part(2, 2, False)
    advance(7, 1)
    dispatch(6)
    last_choice = single_choice(1)
    advance(8, 0)
    advance(8, 1)
    dispatch_single(1, *last_choice)
    far.wait_recv()
    own.last(put_input)
    gram_part(4, 3, False)
    unfold_rows()
    before_sum = len(pending)
    gs.first(lambda blk: gram_rows(7, 1, blk, False))
    for copy in pending[:before_sum]:
        copy.wait_send()
    gs.second()
    gs.last(put_grad)
    for copy in pending[before_sum:]:
        copy.wait_send()
    for copy in saves:
        copy.wait()


def shards(grads, route_weight, routes, hot, expert_inputs):
    inputs = expert_inputs.reshape(EXPERTS * 2, CAP, HIDDEN)
    hbm = pl.BlockSpec(memory_space=pl.ANY)
    dma = pltpu.SemaphoreType.DMA
    hg, hx = WIDTH // NX // 2, HIDDEN // NX // 2
    grad_factor, input_factor = pl.pallas_call(
        kernel,
        out_shape=(
            jax.ShapeDtypeStruct((WIDTH // NX, 1, WIDTH), F32),
            jax.ShapeDtypeStruct((HIDDEN // NX, 1, HIDDEN), F32),
        ),
        in_specs=[hbm] * 5,
        out_specs=(hbm, hbm),
        scratch_shapes=[
            pltpu.VMEM((TOP, TOK), jnp.int32),
            pltpu.VMEM((TOP, TOK), F32),
            pltpu.VMEM((1, EXPERTS), jnp.int32),
            pltpu.VMEM((TOK, WIDTH), BF16),
            pltpu.VMEM((WIDTH // NX, WIDTH), F32),
            pltpu.VMEM((HIDDEN // NX, HIDDEN), F32),
            dma((4,)),
            pltpu.VMEM((EXPERTS * 2, CAP, HIDDEN), BF16),
            pltpu.VMEM((EXPERTS * SLOTS, HIDDEN), BF16),
            dma((5,)),
            pltpu.VMEM((HALF, 2 * TOK, WIDTH), BF16),
            pltpu.VMEM((NZ, 1, TOK), F32),
            pltpu.VMEM((NZ, 1, TOK), F32),
            pltpu.VMEM((2, EXPERTS * SLOTS, TOK), BF16),
            pltpu.VMEM((GROUP, NZ, TOK), F32),
            pltpu.VMEM((GROUP, NZ, TOK), F32),
            pltpu.VMEM((HALF, GROUP, 2 * SLOTS, WIDTH), BF16),
            pltpu.VMEM((HALF, GROUP, 2 * SLOTS, WIDTH), BF16),
            pltpu.VMEM((2, GROUP, 2 * SLOTS, WIDTH // 2), BF16),
            pltpu.VMEM((2, GROUP, 2 * SLOTS, WIDTH // 2), BF16),
            dma((2, GROUP)), dma((2, GROUP)),
            pltpu.VMEM((WIDTH, WIDTH), F32),
            pltpu.VMEM((HIDDEN, HIDDEN), F32),
            pltpu.VMEM((HIDDEN, HIDDEN), F32),
            pltpu.VMEM((2 * hx, HIDDEN), BF16),
            pltpu.VMEM((2 * hx, HIDDEN), BF16),
            pltpu.VMEM((6, hg, WIDTH), BF16),
            pltpu.VMEM((2, hg, WIDTH), BF16),
            pltpu.VMEM((2 * hg, WIDTH), BF16),
            pltpu.VMEM((2 * hg, WIDTH), BF16),
            pltpu.VMEM((6, hx, HIDDEN), BF16),
            pltpu.VMEM((2, hx, HIDDEN), BF16),
            pltpu.VMEM((2 * hx, HIDDEN), BF16),
            pltpu.VMEM((2 * hx, HIDDEN), BF16),
            pltpu.VMEM((6, hx, HIDDEN), BF16),
            pltpu.VMEM((2, hx, HIDDEN), BF16),
            pltpu.VMEM((2 * hx, HIDDEN), BF16),
            pltpu.VMEM((2 * hx, HIDDEN), BF16),
            dma((2, HALF, 2)), dma((2, HALF, 2)),
            dma((NZ,)), dma((NZ,)),
            dma((2,)),
            dma((GROUP,)), dma((GROUP,)),
            dma((HALF, GROUP)), dma((HALF, GROUP)),
            dma((6,)), dma((6,)), dma((6,)), dma((6,)), dma((6,)), dma((6,)),
        ],
        compiler_params=pltpu.CompilerParams(
            collective_id=0, has_side_effects=True, vmem_limit_bytes=60 * 1024 * 1024
        ),
    )(routes.T, route_weight.T, hot.reshape(1, EXPERTS), grads, inputs)
    return input_factor, grad_factor


def solution(mesh):
    return jax.shard_map(
        shards,
        mesh=mesh,
        in_specs=(
            P(("dp", "expert"), None),
            P(("dp", "expert"), None),
            P(("dp", "expert"), None),
            P(),
            P("dp", "expert", None, None, None, None, None),
        ),
        out_specs=(P("dp", "expert", None), P("dp", "expert", None)),
        check_vma=False,
    )
```
